768 devices in a mesh: group: 12 (over z), member: 4 (over x), dp: 16 (over y, core).
Axes of the slice: x: 4, y: 8, z: 12, core: 2. Of those that a mesh axis runs over, the one named last changes fastest.
Arguments:
- tokens_in: bfloat16 [4608, 5120], P(('group', 'member')), may hold values from -6 to 6
- out_grad: bfloat16 [4608, 5120], P(('group', 'member')), may hold values from -6 to 6
- scores: bfloat16 [4608, 6], P(('group', 'member')), may hold values from 0.049804688 to 0.5
- expert_ids: int32 [4608, 6], P(('group', 'member')), may hold values from 0 to 95, as said below
- w_in: bfloat16 [192, 2, 384, 5120], P(('group', 'dp'), None, 'member'), may hold values from -0.078125 to 0.078125
- w_down: bfloat16 [192, 384, 5120], P(('group', 'dp'), 'member'), may hold values from -0.21875 to 0.21875
Outputs:
- grad_in: bfloat16 [4608, 5120], P(('group', 'member'), 'dp')
The draws below stay inside these ranges and needn't reach their ends.
Inputs may be any that keep to these rules, and one draw needn't show every extreme that they name: `expert_ids`: expert E lies in group E // 8. Take the tokens in aligned blocks of 96 (the tokens of one index of group and member). A token's 6 ids name 3 distinct groups, 2 distinct experts in each. Within a block every group is picked by exactly 24 tokens, no expert by more than 6 tokens, and some expert by exactly 6.
All inputs are finite; a program needn't handle non-finite values.
Results may differ from the reference program's by a relative error of at most 0.015.
Values may be sent and summed in bfloat16 or wider, within the bound.
No kernel may reach another device: no remote copies, remote signals or barrier semaphores. Data moves between devices by JAX's collectives and lax.ppermute only.
A program may use at most 32 MiB of HBM per device.

```python
import math
import jax
import jax.numpy as jnp
from jax import lax

D = 5120
H = 768
TOP = 6
TGROUPS = 3
TOK_DEV = 96
SPLIT = 2
EPG = 8
EXPERTS = 96
TOKENS = 4608
ROWS_GROUP = 24
CAP = 6
N_GROUP = 12
N_MEMBER = 4


def draw_expert_ids(key, part):
    key = jax.random.fold_in(key, 7)
    block_count = N_GROUP * N_MEMBER
    first_key, second_key = jax.random.split(key)
    group_score = jax.random.randint(first_key, (block_count, N_GROUP), 0, 1 << 20) * N_GROUP + jnp.arange(N_GROUP, dtype=jnp.int32)[None, :]
    group_perm = jnp.argsort(group_score, axis=1, stable=True).astype(jnp.int32)
    member_score = jax.random.randint(second_key, (block_count, N_GROUP, EPG), 0, 1 << 20) * EPG + jnp.arange(EPG, dtype=jnp.int32)[None, None, :]
    member_perm = jnp.argsort(member_score, axis=2, stable=True).astype(jnp.int32)
    token_pos = jnp.arange(TOK_DEV, dtype=jnp.int32)[:, None] * TGROUPS + jnp.arange(TGROUPS, dtype=jnp.int32)[None, :]
    chosen_group = group_perm[:, token_pos % N_GROUP]
    group_rank = token_pos // N_GROUP
    pair_count = TOP // TGROUPS
    span_count = (pair_count * ROWS_GROUP + CAP - 1) // CAP
    member_pos = (pair_count * group_rank[:, :, None] + jnp.arange(pair_count, dtype=jnp.int32)[None, None, :]) % span_count
    block_index = jnp.arange(block_count, dtype=jnp.int32)[:, None, None, None]
    chosen_member = member_perm[block_index, chosen_group[:, :, :, None], member_pos[None, :, :, :]]
    expert_id = chosen_group[:, :, :, None] * EPG + chosen_member
    return expert_id.reshape(TOKENS, TOP).astype(jnp.int32)


def levels(stream_key, shape, cuts, low, largest):
    loudness = 1.0
    for axis_at, shards_of in cuts:
        steps = jax.random.uniform(jax.random.fold_in(jax.random.fold_in(stream_key, 6), axis_at), (shards_of,), jnp.float32, low / len(cuts), largest / len(cuts))
        loudness = loudness * jnp.repeat(jnp.exp(steps), shape[axis_at] // shards_of).reshape((-1,) + (1,) * (len(shape) - 1 - axis_at))
    return loudness


def noise(stream_key, extent, spread, limit, cuts=(), kind=jnp.bfloat16):
    result = spread * jax.random.normal(stream_key, extent, jnp.float32)
    if cuts:
        result = result * levels(stream_key, extent, cuts, -0.22, 0.18)
    return jnp.clip(result, -limit, limit).astype(kind)


def setup_inputs(seed: int = 0) -> dict:
    arg_keys = jax.random.split(jax.random.key(seed), 7)
    return {
        "tokens_in": noise(arg_keys[0], (TOKENS, D), 1.0, 6.0, ((0, 48),)),
        "out_grad": noise(arg_keys[1], (TOKENS, D), 1.0, 6.0, ((0, 48),)),
        "scores": jnp.clip(jnp.exp(math.log(0.5) - 2.306499 * jax.random.uniform(arg_keys[2], (TOKENS, TOP), jnp.float32) ** levels(arg_keys[2], (TOKENS, TOP), ((0, 48),), -0.2, 0.2)), 0.049804688, 0.5).astype(jnp.bfloat16),
        "expert_ids": draw_expert_ids(jax.random.fold_in(arg_keys[6], 71), 0),
        "w_in": noise(arg_keys[4], (EXPERTS * SPLIT, 2, H // SPLIT, D), D ** -0.5, 0.078125, ((0, 192), (2, 4))),
        "w_down": noise(arg_keys[5], (EXPERTS * SPLIT, H // SPLIT, D), H ** -0.5, 0.21875, ((0, 192), (1, 4))),
    }


def reference(tokens_in, out_grad, scores, expert_ids, w_in, w_down):
    flat_ids = expert_ids.reshape(-1).astype(jnp.int32)
    order = jnp.argsort(flat_ids, stable=True).astype(jnp.int32)
    capacity_all = N_GROUP * N_MEMBER * CAP
    padded_order = jnp.concatenate([order, jnp.zeros((capacity_all,), jnp.int32)])
    expert_range = jnp.arange(EXPERTS, dtype=jnp.int32)
    counts = jnp.sum((flat_ids[None, :] == expert_range[:, None]).astype(jnp.int32), axis=1)
    starts = (jnp.cumsum(counts) - counts).astype(jnp.int32)
    score_flat = scores.reshape(-1).astype(jnp.float32)
    model_width = tokens_in.shape[1]
    part_hidden = w_in.shape[2]
    block_hidden = part_hidden // N_MEMBER
    w_in_split = w_in.reshape(EXPERTS, SPLIT, 2, part_hidden, model_width)
    w_down_split = w_down.reshape(EXPERTS, SPLIT * part_hidden, model_width)

    def per_expert(accum, items):
        expert, w_parts, w_out = items
        start = starts[expert]
        picks = lax.dynamic_slice(padded_order, (start,), (capacity_all,))
        valid = jnp.arange(capacity_all, dtype=jnp.int32) < counts[expert]
        token_index = (picks // TOP).astype(jnp.int32)
        inputs = tokens_in[token_index]
        grads = out_grad[token_index].astype(jnp.float32)
        weight_rows = jnp.where(valid, score_flat[picks], 0.0)
        scaled = (weight_rows[:, None] * grads).astype(jnp.bfloat16)
        gate_full = w_parts[:, 0].reshape(SPLIT * part_hidden, model_width)
        up_full = w_parts[:, 1].reshape(SPLIT * part_hidden, model_width)
        gate_pre = jnp.dot(inputs, gate_full.T, preferred_element_type=jnp.float32)
        up_pre = jnp.dot(inputs, up_full.T, preferred_element_type=jnp.float32)
        act_grad = jnp.dot(scaled, w_out.T, preferred_element_type=jnp.float32)
        sigmoid_gate = jax.nn.sigmoid(gate_pre)
        gate_grad = (act_grad * up_pre * sigmoid_gate * (1.0 + gate_pre * (1.0 - sigmoid_gate))).astype(jnp.bfloat16)
        up_grad = (act_grad * gate_pre * sigmoid_gate).astype(jnp.bfloat16)
        gate_blocks = gate_grad.astype(jnp.float32).reshape(capacity_all, SPLIT, N_MEMBER, block_hidden)
        up_blocks = up_grad.astype(jnp.float32).reshape(capacity_all, SPLIT, N_MEMBER, block_hidden)
        gate_weight = gate_full.astype(jnp.float32).reshape(SPLIT, N_MEMBER, block_hidden, model_width)
        up_weight = up_full.astype(jnp.float32).reshape(SPLIT, N_MEMBER, block_hidden, model_width)
        partial_value = jnp.einsum("rsnh,snhd->snrd", gate_blocks, gate_weight) + jnp.einsum("rsnh,snhd->snrd", up_blocks, up_weight)
        rounded = lax.optimization_barrier(partial_value.astype(jnp.bfloat16))
        part_grad = jnp.sum(rounded.astype(jnp.float32), axis=1).astype(jnp.bfloat16)
        part_grad = lax.optimization_barrier(part_grad)
        pick_sum = jnp.sum(part_grad.astype(jnp.float32), axis=0)
        contribution = jnp.where(valid[:, None], pick_sum, 0.0)
        accum = accum.at[token_index].add(contribution)
        return accum, None

    start_accum = jnp.zeros(tokens_in.shape, jnp.float32)
    total, unused = lax.scan(per_expert, start_accum, (expert_range, w_in_split, w_down_split))
    return total.astype(jnp.bfloat16)
```

```python
import jax
import jax.numpy as jnp
from jax import lax
from jax.experimental import pallas as pl
from jax.experimental.pallas import tpu as pltpu
from jax.sharding import Mesh, PartitionSpec as P

TGROUPS = 3
QUARTERS = 4
LANES = 128
INTERPRET = False
F32 = jnp.float32
BF16 = jnp.bfloat16


def iota(shape, dim):
    return lax.broadcasted_iota(jnp.int32, shape, dim)


def call(body, out_shape, *args, scratch=(), smem=0, flops=0):
    specs = [
        pl.BlockSpec(memory_space=pltpu.SMEM if i < smem else pltpu.VMEM) for i in range(len(args))
    ]
    moved = sum(a.size * a.dtype.itemsize for a in args)
    return pl.pallas_call(
        body,
        out_shape=out_shape,
        in_specs=specs,
        out_specs=jax.tree.map(lambda s: pl.BlockSpec(memory_space=pltpu.VMEM), out_shape),
        scratch_shapes=list(scratch),
        compiler_params=pltpu.CompilerParams(vmem_limit_bytes=40 * 1024 * 1024),
        cost_estimate=pl.CostEstimate(flops=flops, bytes_accessed=moved, transcendentals=0),
        interpret=INTERPRET,
    )(*args)


def dot(a, b):
    return jnp.dot(a, b, preferred_element_type=F32)


def dot_last(a, b):
    return lax.dot_general(a, b, (((1,), (1,)), ((), ())), preferred_element_type=F32)


def picked(ids, target):
    hit = jnp.zeros(target.shape, F32)
    for e in range(ids.shape[0]):
        hit += (ids[e : e + 1, :] == target).astype(F32)
    return hit


def before(tokens, lanes):
    return (iota((tokens, lanes), 0) < iota((tokens, lanes), 1) % tokens).astype(BF16)


def slot_matrix(ids, y, groups, per_group, slots):
    tokens = ids.shape[1]
    lanes = QUARTERS * tokens
    rows_each = QUARTERS * slots
    rows = groups * rows_each
    hit = picked(ids, iota((groups, tokens), 0) * per_group + y).astype(BF16)
    same = (iota((tokens, lanes), 0) == iota((tokens, lanes), 1) % tokens).astype(BF16)
    rank = dot(hit, before(tokens, lanes))
    hit4 = dot(hit, same)
    code = jnp.where(hit4 > 0.5, rank, -1.0).astype(BF16)
    expand = (iota((rows, groups), 0) // rows_each == iota((rows, groups), 1)).astype(BF16)
    row = iota((rows, lanes), 0) % rows_each
    spread = dot(expand, code).astype(jnp.int32)
    mark = (spread == row % slots) & (row // slots == iota((rows, lanes), 1) // tokens)
    return mark, expand, same


def stacked_quarters(ref, core, half):
    quarter = half // QUARTERS
    return jnp.concatenate(
        [
            ref[:, pl.ds(pl.multiple_of(core * half + f * quarter, LANES), quarter)]
            for f in range(QUARTERS)
        ],
        axis=0,
    )


def pack_inputs(groups, per_group, slots, info, ids, tokens, out):
    mark, _, _ = slot_matrix(ids[...], info[0], groups, per_group, slots)
    rows = stacked_quarters(tokens, info[1], tokens.shape[1] // 2)
    out[...] = dot(mark.astype(BF16), rows).astype(BF16)


def pack_grads(groups, per_group, slots, info, ids, scores, grads, out):
    ids_now = ids[...]
    mark, expand, same = slot_matrix(ids_now, info[0], groups, per_group, slots)
    tokens = ids_now.shape[1]
    target = iota((groups, tokens), 0) * per_group + info[0]
    score = jnp.zeros((groups, tokens), F32)
    for e in range(ids_now.shape[0]):
        score += jnp.where(ids_now[e : e + 1, :] == target, scores[e : e + 1, :].astype(F32), 0.0)
    wide = dot(expand, dot(score.astype(BF16), same).astype(BF16))
    slot_score = jnp.sum(jnp.where(mark, wide, 0.0), axis=1, keepdims=True)
    rows = stacked_quarters(grads, info[1], grads.shape[1] // 2)
    out[...] = (slot_score * dot(mark.astype(BF16), rows)).astype(BF16)


def group_codes(ids, per_group, groups):
    tokens = ids.shape[1]
    hit = picked(ids // per_group, iota((groups, tokens), 0)) > 0.5
    rank = dot(hit.astype(BF16), before(tokens, tokens))
    return jnp.where(hit, rank, -1.0)


def describe(groups, per_group, slots, rows_group, ids, ranks, gather):
    ids_now = ids[...]
    tokens = ids_now.shape[1]
    experts = groups * per_group
    codes = group_codes(ids_now, per_group, groups).astype(BF16)
    hit = picked(ids_now, iota((experts, tokens), 0)) > 0.5
    order = dot(hit.astype(BF16), before(tokens, tokens))
    widen = (iota((experts, groups), 0) // per_group == iota((experts, groups), 1)).astype(BF16)
    rank = dot(widen, codes)
    lane = iota((experts, LANES), 1)
    result = jnp.zeros((experts, LANES), F32)
    for r in range(slots):
        value = jnp.sum(jnp.where(hit & (order == r), rank, 0.0), axis=1, keepdims=True)
        result += jnp.where(lane == r, value, 0.0)
    ranks[...] = result.astype(jnp.int32)
    rows = groups * rows_group
    expand = (iota((rows, groups), 0) // rows_group == iota((rows, groups), 1)).astype(BF16)
    spread = dot(expand, codes).astype(jnp.int32)
    gather[...] = (spread == iota((rows, tokens), 0) % rows_group).astype(BF16)


def unpack(slots, x, rows):
    piece = 8 * QUARTERS * slots
    each = 8 * slots
    at = iota((piece, piece), 0)
    source = (at % each) // slots * (QUARTERS * slots) + at // each * slots + at % slots
    order = (source == iota((piece, piece), 1)).astype(BF16)
    for i in range(x.shape[0] // piece):
        moved = dot(order, x[i * piece : (i + 1) * piece, :]).astype(BF16)
        for f in range(QUARTERS):
            rows[f, i * each : (i + 1) * each, :] = moved[f * each : (f + 1) * each, :]


def project(slots, info, x, own, other, out, rows):
    unpack(slots, x, rows)
    half = other.shape[1]
    quarter = half // QUARTERS
    width = other.shape[0]
    mine = jnp.zeros((rows.shape[1], width), F32)
    theirs = jnp.zeros((rows.shape[1], width), F32)
    for f in range(QUARTERS):
        begin = pl.multiple_of(info[1] * half + f * quarter, LANES)
        mine += dot_last(rows[f], own[:, pl.ds(begin, quarter)])
        theirs += dot_last(rows[f], other[:, f * quarter : (f + 1) * quarter])
    out[0] = mine
    out[1] = theirs


def backward(pre, pre_far, act, act_far, own, other, out):
    hidden = act.shape[2]
    grads = []
    for s in range(2):
        both = pre[s] + pre_far[1 - s]
        gate, up = both[:, :hidden], both[:, hidden:]
        slope = act[s] + act_far[1 - s]
        sig = jax.nn.sigmoid(gate)
        gate_grad = slope * up * sig * (1.0 + gate * (1.0 - sig))
        up_grad = slope * gate * sig
        grads.append((gate_grad.astype(BF16), up_grad.astype(BF16)))
    step = 640 if out.shape[1] % 640 == 0 else out.shape[1]
    for j in range(out.shape[1] // step):
        at = slice(j * step, (j + 1) * step)
        total = dot(grads[0][0], own[:hidden, at]) + dot(grads[0][1], own[hidden:, at])
        total += dot(grads[1][0], other[:hidden, at]) + dot(grads[1][1], other[hidden:, at])
        out[:, at] = total.astype(BF16)


def windows(chunk, count):
    starts = [chunk * k // LANES * LANES for k in range(count)]
    ends = [-(-(chunk * (k + 1)) // LANES) * LANES for k in range(count)]
    return starts, max(e - s for s, e in zip(starts, ends))


def add_members(starts, width, x, out):
    for k, begin in enumerate(starts):
        at = slice(begin, begin + width)
        total = x[0, :, at].astype(F32)
        for m in range(1, x.shape[0]):
            total += x[m, :, at].astype(F32)
        out[k] = total.astype(BF16)


def merge(codes, x, out):
    mark = (codes[...] == iota((out.shape[0], x.shape[0]), 0)).astype(BF16)
    out[...] = dot(mark, x[...]).astype(BF16)


def finish(gather, x, out):
    out[...] = lax.dot_general(
        gather[...], x[...], (((0,), (0,)), ((), ())), preferred_element_type=F32
    ).astype(BF16)


def per_device(tokens_in, out_grad, scores, expert_ids, w_in, w_down):
    groups, members = lax.axis_size("group"), lax.axis_size("member")
    columns = lax.axis_size("y")
    y, core = lax.axis_index("y"), lax.axis_index("core")
    tokens, width = tokens_in.shape
    picks = expert_ids.shape[1]
    pairs = picks // TGROUPS
    per_group = columns
    rows_group = TGROUPS * tokens // groups
    slots = pairs * rows_group // per_group
    half = width // 2
    quarter = half // QUARTERS
    chunk = width // (2 * columns)
    hidden = w_down.shape[1]
    packed_rows = groups * QUARTERS * slots
    all_rows = members * groups * slots
    swap = [(0, 1), (1, 0)]

    def struct(shape, kind):
        return jax.ShapeDtypeStruct(shape, kind)

    def exchange(x, axis):
        return lax.all_to_all(x, axis, split_axis=0, concat_axis=0, tiled=True)

    def to_group(x):
        return exchange(x.reshape(groups, -1, x.shape[1]), "group").reshape(x.shape)

    def to_members(x):
        copies = jnp.broadcast_to(x[None], (members,) + x.shape)
        return exchange(copies, "member").reshape(members * x.shape[0], x.shape[1])

    info = jnp.stack([y, core]).astype(jnp.int32)
    ids = expert_ids.T
    sizes = (groups, per_group, slots)

    def bind(body, *front):
        return lambda *refs: body(*front, *refs)

    packed = struct((packed_rows, quarter), BF16)
    sent_in = call(bind(pack_inputs, *sizes), packed, info, ids, tokens_in, smem=1)
    near_in = to_group(sent_in)
    sent_grad = call(bind(pack_grads, *sizes), packed, info, ids, scores.T, out_grad, smem=1)
    near_grad = to_group(sent_grad)
    ranks, gather = call(
        bind(describe, *sizes, rows_group),
        (
            struct((groups * per_group, LANES), jnp.int32),
            struct((groups * rows_group, tokens), BF16),
        ),
        ids,
    )
    ranks = to_group(ranks).reshape(groups, per_group, LANES)[:, :, :slots]
    ranks += rows_group * jnp.arange(groups, dtype=jnp.int32)[:, None, None]
    codes = ranks.transpose(1, 0, 2).reshape(1, -1)

    w_pair = w_in[0].reshape(2 * hidden, width)
    w_out = w_down[0]

    def far(x):
        return lax.ppermute(x, "core", swap)

    pair_far = far(lax.dynamic_slice_in_dim(w_pair, (1 - core) * half, half, axis=1))
    out_far = far(lax.dynamic_slice_in_dim(w_out, (1 - core) * half, half, axis=1))
    by_chunk = w_pair.reshape(2 * hidden, columns, 2, chunk)
    back_own = lax.dynamic_index_in_dim(by_chunk, core, 2, keepdims=False)
    back_own = back_own.reshape(2 * hidden, half)
    back_far = lax.dynamic_index_in_dim(by_chunk, 1 - core, 2, keepdims=False)
    back_far = far(back_far.reshape(2 * hidden, half))

    scratch = (pltpu.VMEM((QUARTERS, all_rows, quarter), BF16),)
    rows_in = to_members(near_in)
    pre = call(
        bind(project, slots),
        struct((2, all_rows, 2 * hidden), F32),
        info, rows_in, w_pair, pair_far,
        scratch=scratch, smem=1,
    )
    pre_far = far(pre)
    rows_grad = to_members(near_grad)
    act = call(
        bind(project, slots),
        struct((2, all_rows, hidden), F32),
        info, rows_grad, w_out, out_far,
        scratch=scratch, smem=1,
    )
    act_far = far(act)
    partial = call(
        backward, struct((all_rows, half), BF16), pre, pre_far, act, act_far, back_own, back_far
    )

    arrived = exchange(partial.reshape(members, groups * slots, half), "member")
    starts, window = windows(chunk, columns)
    summed = call(
        bind(add_members, starts, window),
        struct((columns, groups * slots, window), BF16),
        arrived,
    )
    summed = exchange(summed, "y").reshape(columns * groups * slots, window)
    merged = call(merge, struct((groups * rows_group, window), BF16), codes, summed)
    returned = to_group(merged)
    result = call(finish, struct((tokens, window), BF16), gather, returned)
    begin = y * chunk % LANES
    return lax.dynamic_slice_in_dim(result, begin, chunk, axis=1)


def solution(mesh):
    shape = mesh.devices.shape
    split = Mesh(
        mesh.devices.reshape(shape[0], shape[1], shape[2] // 2, 2),
        ("group", "member", "y", "core"),
    )
    in_specs = (
        P(("group", "member"), None),
        P(("group", "member"), None),
        P(("group", "member"), None),
        P(("group", "member"), None),
        P(("group", "y", "core"), None, "member", None),
        P(("group", "y", "core"), "member", None),
    )
    out_specs = P(("group", "member"), ("y", "core"))
    return jax.shard_map(
        per_device, mesh=split, in_specs=in_specs, out_specs=out_specs, check_vma=False
    )
```

```python
import jax
import jax.numpy as jnp
from jax import lax
from jax.experimental import pallas as pl
from jax.experimental.pallas import tpu as pltpu
from jax.sharding import Mesh, PartitionSpec as P

TGROUPS = 3
QUARTERS = 4
LANES = 128
INTERPRET = False
F32 = jnp.float32
BF16 = jnp.bfloat16


def iota(shape, dim):
    return lax.broadcasted_iota(jnp.int32, shape, dim)


def call(body, out_shape, *args, scratch=(), smem=0, far=(), flops=0, room=40):
    def place(i):
        if i < smem:
            return pl.BlockSpec(memory_space=pltpu.SMEM)
        return pl.BlockSpec(memory_space=pltpu.HBM if i in far else pltpu.VMEM)

    moved = sum(a.size * a.dtype.itemsize for a in args)
    return pl.pallas_call(
        body,
        out_shape=out_shape,
        in_specs=[place(i) for i in range(len(args))],
        out_specs=jax.tree.map(lambda s: pl.BlockSpec(memory_space=pltpu.VMEM), out_shape),
        scratch_shapes=list(scratch),
        compiler_params=pltpu.CompilerParams(vmem_limit_bytes=room * 1024 * 1024),
        cost_estimate=pl.CostEstimate(flops=flops, bytes_accessed=moved, transcendentals=0),
        interpret=INTERPRET,
    )(*args)


def dot(a, b):
    return jnp.dot(a, b, preferred_element_type=F32)


def dot_last(a, b):
    return lax.dot_general(a, b, (((1,), (1,)), ((), ())), preferred_element_type=F32)


def dot_first(a, b):
    return lax.dot_general(a, b, (((0,), (0,)), ((), ())), preferred_element_type=F32)


def picked(ids, target):
    hit = jnp.zeros(target.shape, F32)
    for e in range(ids.shape[0]):
        hit += (ids[e : e + 1, :] == target).astype(F32)
    return hit


def before(tokens, lanes):
    return (iota((tokens, lanes), 0) < iota((tokens, lanes), 1) % tokens).astype(BF16)


def slot_matrix(ids, y, groups, per_group, slots):
    tokens = ids.shape[1]
    lanes = QUARTERS * tokens
    rows_each = QUARTERS * slots
    rows = groups * rows_each
    hit = picked(ids, iota((groups, tokens), 0) * per_group + y).astype(BF16)
    same = (iota((tokens, lanes), 0) == iota((tokens, lanes), 1) % tokens).astype(BF16)
    rank = dot(hit, before(tokens, lanes))
    hit4 = dot(hit, same)
    code = jnp.where(hit4 > 0.5, rank, -1.0).astype(BF16)
    expand = (iota((rows, groups), 0) // rows_each == iota((rows, groups), 1)).astype(BF16)
    row = iota((rows, lanes), 0) % rows_each
    spread = dot(expand, code).astype(jnp.int32)
    mark = (spread == row % slots) & (row // slots == iota((rows, lanes), 1) // tokens)
    return mark, expand, same


def stacked_quarters(ref):
    quarter = ref.shape[1] // QUARTERS
    return jnp.concatenate(
        [ref[:, f * quarter : (f + 1) * quarter] for f in range(QUARTERS)], axis=0
    )


def pack(groups, per_group, slots, info, *refs):
    sources, out, held, done = refs[:4], refs[4], refs[5:9], refs[9]
    ids, scores, near_tokens, near_grads = held
    half = near_tokens.shape[1]
    lanes = pl.ds(pl.multiple_of(info[1] * half, LANES), half)
    copies = []
    for n, (source, target) in enumerate(zip(sources, held)):
        source = source.at[:, lanes] if n >= 2 else source
        copies.append(pltpu.make_async_copy(source, target, done.at[n]))
    for copy in copies:
        copy.start()
    copies[0].wait()
    copies[1].wait()
    ids_now = ids[...]
    mark, expand, same = slot_matrix(ids_now, info[0], groups, per_group, slots)
    target = iota((groups, ids_now.shape[1]), 0) * per_group + info[0]
    score = jnp.zeros(target.shape, F32)
    for e in range(ids_now.shape[0]):
        score += jnp.where(ids_now[e : e + 1, :] == target, scores[e : e + 1, :].astype(F32), 0.0)
    wide = dot(expand, dot(score.astype(BF16), same).astype(BF16))
    slot_score = jnp.sum(jnp.where(mark, wide, 0.0), axis=1, keepdims=True)
    mark = mark.astype(BF16)
    quarter = half // QUARTERS
    copies[2].wait()
    out[:, :quarter] = dot(mark, stacked_quarters(near_tokens)).astype(BF16)
    copies[3].wait()
    out[:, quarter:] = (slot_score * dot(mark, stacked_quarters(near_grads))).astype(BF16)


ENTRIES = ((0, 0), (0, 1), (0, 2), (1, 2), (1, 3), (1, 4))
PIECE = 16


def describe(groups, per_group, slots, pad, ids, gather, place, order):
    ids_now = ids[...]
    tokens = ids_now.shape[1]
    experts = groups * per_group
    hit = picked(ids_now, iota((experts, tokens), 0)) > 0.5
    rank = dot(hit.astype(BF16), before(tokens, tokens))
    code = jnp.where(hit, rank, -1.0).astype(BF16)
    lanes = experts * PIECE
    widen = (iota((experts, lanes), 1) // PIECE == iota((experts, lanes), 0)).astype(BF16)
    spread = dot_first(code, widen).astype(jnp.int32)
    row = iota((tokens, lanes), 1) % PIECE
    for n, (odd, part) in enumerate(ENTRIES):
        mark = (spread == 2 * (row % 3) + odd) & (row // 3 == part)
        gather[n * tokens : (n + 1) * tokens, :] = mark.astype(BF16)

    rows = groups * slots
    at, col = iota(place.shape, 0), iota(place.shape, 1)
    row, source = at % PIECE, col % rows
    mark = jnp.zeros(place.shape, jnp.bool_)
    for n, (odd, part) in enumerate(ENTRIES):
        mark |= (col // rows == n) & (row // 3 == part) & (source % slots == 2 * (row % 3) + odd)
    place[...] = (mark & (at // PIECE == source // slots)).astype(BF16)

    at = iota(order.shape[1:], 0)
    inner = at % pad
    source = inner // slots * (QUARTERS * slots) + at // pad * slots + inner % slots
    for h in range(2):
        here = iota(order.shape[1:], 1) + h * order.shape[2]
        order[h] = ((source == here) & (inner < rows)).astype(BF16)


def round_up(n, k):
    return -(-n // k) * k


def project(blocks, whole, info, order, *refs):
    parts, (pair, pair_far, down, down_far, out, ins, grads) = refs[:-7], refs[-7:]
    quarter = ins.shape[2]
    pad = ins.shape[1] // blocks
    middle = order.shape[2]
    halves = []
    if whole:
        halves += [parts[0][:middle, :], parts[0][middle:, :]]
    halves += [p[...] for p in parts[whole:]]
    for k in range(blocks):
        moved = dot(order[0], halves[2 * k]) + dot(order[1], halves[2 * k + 1])
        moved = moved.astype(BF16)
        for f in range(QUARTERS):
            at = slice(f * pad, (f + 1) * pad)
            ins[f, k * pad : (k + 1) * pad, :] = moved[at, :quarter]
            grads[f, k * pad : (k + 1) * pad, :] = moved[at, quarter:]
    half = QUARTERS * quarter
    hidden = down.shape[0]
    for rows, own, far, begin in ((ins, pair, pair_far, 0), (grads, down, down_far, 2 * LANES)):
        for s, weight in enumerate((own, far)):
            total = jnp.zeros((ins.shape[1], weight.shape[0]), F32)
            for f in range(QUARTERS):
                lanes = pl.ds(pl.multiple_of(info[1] * half + f * quarter, LANES), quarter)
                total += dot_last(rows[f], weight[:, lanes])
            out[s, :, begin : begin + weight.shape[0]] = total


def backward(info, pre_a, got_a, pre_b, got_b, own, far, out):
    hidden = own.shape[0] // 2
    grads = []
    for s in range(2):
        total = jnp.concatenate([pre_a[s] + got_a[1 - s], pre_b[s] + got_b[1 - s]], axis=0)
        gate, up = total[:, :hidden], total[:, hidden : 2 * hidden]
        slope = total[:, 2 * LANES : 2 * LANES + hidden]
        sig = jax.nn.sigmoid(gate)
        gate_grad = slope * up * sig * (1.0 + gate * (1.0 - sig))
        up_grad = slope * gate * sig
        grads.append(jnp.concatenate([gate_grad, up_grad], axis=1).astype(BF16))
    first_core = info[1] == 0
    members = out.shape[0]
    count = grads[0].shape[0]
    pad = count // members
    window = 3 * LANES
    chunk = own.shape[1] // 16
    block_rows = out.shape[1] * LANES // (8 * chunk)
    low = iota((count, LANES), 1) < LANES // 2
    for f in range(4):
        pair = []
        for y in (2 * f, 2 * f + 1):
            lanes = pl.ds(pl.multiple_of(2 * chunk * y + 2 * LANES * info[1], LANES), window)
            pair.append(dot(grads[0], own[:, lanes]) + dot(grads[1], far[:, lanes]))
        turned = jnp.where(first_core, pair[1], pair[0])
        turned = pltpu.roll(turned, jnp.where(first_core, LANES // 2, window - LANES // 2), 1)
        even = jnp.where(first_core, pair[0], turned)
        odd = jnp.where(first_core, turned, pair[1])
        seam = jnp.where(low, even[:, 2 * LANES :], odd[:, :LANES])
        tiles = [even[:, :LANES], even[:, LANES : 2 * LANES], seam]
        tiles += [odd[:, LANES : 2 * LANES], odd[:, 2 * LANES :]]
        for t, tile in enumerate(tiles):
            begin = (5 * f + t) * block_rows
            for k, shift in enumerate((0, members - 1, 1, 2)):
                home = lax.rem(info[2] + shift, members)
                out[home, begin : begin + block_rows, :] = tile[
                    k * pad : k * pad + block_rows
                ].astype(BF16)


def total_pieces(groups, columns, place, x, out):
    rows = place.shape[1] // len(ENTRIES)
    low = iota((rows, LANES), 1) < LANES // 2
    for y in range(columns):
        tiles, turned = [], []
        for t in range(3):
            at = (5 * y // 2 + t) * rows
            tile = x[0, at : at + rows, :].astype(F32)
            for m in range(1, x.shape[0]):
                tile += x[m, at : at + rows, :].astype(F32)
            tiles.append(tile)
            turned.append(pltpu.roll(tile, LANES // 2, 1))
        first = [
            jnp.where(low, turned[0], turned[1]),
            jnp.where(low, turned[1], turned[2]),
        ]
        if y % 2 == 0:
            entries = tiles[:2] + [jnp.where(low, tiles[2], 0.0), jnp.where(low, 0.0, turned[0])] + first
        else:
            entries = first + [jnp.where(low, turned[2], 0.0), jnp.where(low, 0.0, tiles[0])] + tiles[1:]
        stack = jnp.concatenate(entries, axis=0).astype(BF16)
        moved = dot(place[...], stack).astype(BF16)
        for g in range(groups):
            out[g * columns + y] = moved[g * PIECE : (g + 1) * PIECE]


def finish(gather, x, out):
    tokens, chunk = out.shape
    found = dot(gather[...], x[...])
    part = [found[n * tokens : (n + 1) * tokens] for n in range(len(ENTRIES))]
    turned = [pltpu.roll(p, LANES // 2, 1) for p in part[3:]]
    low = iota((tokens, LANES), 1) < LANES // 2
    out[:, :LANES] = (part[0] + jnp.where(low, turned[0], turned[1])).astype(BF16)
    out[:, LANES : 2 * LANES] = (part[1] + jnp.where(low, turned[1], turned[2])).astype(BF16)
    last = (part[2] + turned[2]).astype(BF16)
    out[:, 2 * LANES :] = last[:, : chunk - 2 * LANES]


def per_device(tokens_in, out_grad, scores, expert_ids, w_in, w_down):
    groups, members = lax.axis_size("group"), lax.axis_size("member")
    columns = lax.axis_size("y")
    tokens, width = tokens_in.shape
    picks = expert_ids.shape[1]
    pairs = picks // TGROUPS
    slots = pairs * (TGROUPS * tokens // groups) // columns
    half = width // 2
    quarter = half // QUARTERS
    chunk = width // (2 * columns)
    hidden = w_down.shape[1]
    block_rows = groups * slots
    pad = round_up(block_rows, 16)
    packed_rows = block_rows * QUARTERS
    middle = packed_rows // 2

    def struct(shape, kind):
        return jax.ShapeDtypeStruct(shape, kind)

    def exchange(x, axis):
        return lax.all_to_all(x, axis, split_axis=0, concat_axis=0, tiled=True)

    def up(x):
        return lax.ppermute(x, "member", [(i, (i + 1) % members) for i in range(members)])

    def down(x):
        return lax.ppermute(x, "member", [(i, (i - 1) % members) for i in range(members)])

    def far(x):
        return lax.ppermute(x, "core", [(0, 1), (1, 0)])

    def bind(body, *front):
        return lambda *refs: body(*front, *refs)

    places = [lax.axis_index(name) for name in ("y", "core", "member")]
    info = jnp.stack(places).astype(jnp.int32)
    ids = expert_ids.T
    sent = call(
        bind(pack, groups, columns, slots),
        struct((packed_rows, 2 * quarter), BF16),
        info, ids, scores.T, tokens_in, out_grad,
        smem=1, far=(1, 2, 3, 4), room=60,
        scratch=(
            pltpu.VMEM(ids.shape, ids.dtype),
            pltpu.VMEM(ids.shape, BF16),
            pltpu.VMEM((tokens, half), BF16),
            pltpu.VMEM((tokens, half), BF16),
            pltpu.SemaphoreType.DMA((4,)),
        ),
    )
    w_pair = w_in[0].reshape(2 * hidden, width)
    w_out = w_down[0]
    sent, ids, pair_late, out_late = lax.optimization_barrier((sent, ids, w_pair, w_out))
    near = exchange(sent.reshape(groups, -1, 2 * quarter), "group").reshape(sent.shape)
    pair_far, out_far = far(pair_late), far(out_late)
    gather, place, order = call(
        bind(describe, groups, columns, slots, pad),
        (
            struct((len(ENTRIES) * tokens, groups * columns * PIECE), BF16),
            struct((groups * PIECE, len(ENTRIES) * block_rows), BF16),
            struct((2, QUARTERS * pad, middle), BF16),
        ),
        ids,
    )
    near, order, pair_far, out_far = lax.optimization_barrier((near, order, pair_far, out_far))
    weights = (w_pair, pair_far, w_out, out_far)

    top, bottom = near[:middle], near[middle:]
    below_top, above_bottom = up(top), down(bottom)
    below_bottom, above_top = up(bottom), down(top)
    opposite = (up(below_top), down(above_bottom))

    def step(blocks, *parts):
        count = blocks * pad
        return call(
            bind(project, blocks, blocks == 3),
            struct((2, count, 3 * LANES), F32),
            info, order, *parts, *weights,
            smem=1, flops=12 * count * half * hidden,
            scratch=(
                pltpu.VMEM((QUARTERS, count, quarter), BF16),
                pltpu.VMEM((QUARTERS, count, quarter), BF16),
            ),
        )

    pre_a = step(3, near, below_top, below_bottom, above_top, above_bottom)
    pre_late, *opposite = lax.optimization_barrier((pre_a, *opposite))
    got_a = far(pre_late)
    pre_b = step(1, *opposite)
    got_b = far(pre_b)
    partial = call(
        backward,
        struct((members, block_rows * half // LANES, LANES), BF16),
        info, pre_a, got_a, pre_b, got_b, w_pair, pair_far,
        smem=1, flops=8 * members * pad * hidden * half,
    )
    pieces = call(
        bind(total_pieces, groups, columns),
        struct((groups * columns, PIECE, LANES), BF16),
        place, exchange(partial, "member"),
    )
    arrived = exchange(pieces, ("group", "y")).reshape(-1, LANES)
    return call(finish, struct((tokens, chunk), BF16), gather, arrived)


def solution(mesh):
    shape = mesh.devices.shape
    split = Mesh(
        mesh.devices.reshape(shape[0], shape[1], shape[2] // 2, 2),
        ("group", "member", "y", "core"),
    )
    in_specs = (
        P(("group", "member"), None),
        P(("group", "member"), None),
        P(("group", "member"), None),
        P(("group", "member"), None),
        P(("group", "y", "core"), None, "member", None),
        P(("group", "y", "core"), "member", None),
    )
    out_specs = P(("group", "member"), ("y", "core"))
    return jax.shard_map(
        per_device, mesh=split, in_specs=in_specs, out_specs=out_specs, check_vma=False
    )
```

```python
from types import MappingProxyType

import jax
import jax.numpy as jnp
from jax import lax
from jax.experimental import pallas as pl
from jax.experimental.pallas import tpu as pltpu
from jax.sharding import Mesh, PartitionSpec as P

TGROUPS = 3
PARTS = 8
CORES = 2
LATE = 128
LANES = 128
INTERPRET = False
F32 = jnp.float32
BF16 = jnp.bfloat16


def iota(shape, dim):
    return lax.broadcasted_iota(jnp.int32, shape, dim)


def call(body, out_shape, *args, scratch=(), far=MappingProxyType({}), far_out=False, alias=None, flops=0, room=20):
    moved = sum(a.size * a.dtype.itemsize for a in args)
    target = pl.ANY if far_out else pltpu.VMEM
    return pl.pallas_call(
        body,
        out_shape=out_shape,
        in_specs=[pl.BlockSpec(memory_space=far.get(i, pltpu.VMEM)) for i in range(len(args))],
        out_specs=jax.tree.map(lambda s: pl.BlockSpec(memory_space=target), out_shape),
        scratch_shapes=list(scratch),
        input_output_aliases={} if alias is None else {alias: 0},
        compiler_params=pltpu.CompilerParams(vmem_limit_bytes=room * 1024 * 1024),
        cost_estimate=pl.CostEstimate(flops=flops, bytes_accessed=moved, transcendentals=0),
        interpret=INTERPRET,
    )(*args)


def dot(a, b):
    return jnp.dot(a, b, preferred_element_type=F32)


def dot_last(a, b):
    return lax.dot_general(a, b, (((1,), (1,)), ((), ())), preferred_element_type=F32)


def dot_first(a, b):
    return lax.dot_general(a, b, (((0,), (0,)), ((), ())), preferred_element_type=F32)


def picked(ids, target):
    hit = jnp.zeros(target.shape, F32)
    for e in range(ids.shape[0]):
        hit += (ids[e : e + 1, :] == target).astype(F32)
    return hit


def before(tokens, lanes):
    return (iota((tokens, lanes), 0) < iota((tokens, lanes), 1) % tokens).astype(BF16)


def stacked_parts(ref):
    part = ref.shape[1] // PARTS
    return jnp.concatenate([ref[:, f * part : (f + 1) * part] for f in range(PARTS)], axis=0)


def pack(groups, per_group, slots, ids_far, scores_far, tokens_far, grads_far, out, ids, scores, tokens, grads, done):
    sources, targets = (ids_far, scores_far, tokens_far, grads_far), (ids, scores, tokens, grads)
    copies = [
        pltpu.make_async_copy(source, target, done.at[n])
        for n, (source, target) in enumerate(zip(sources, targets))
    ]
    for copy in copies:
        copy.start()
    count = ids.shape[1]
    lanes = PARTS * count
    own_slots = slots // CORES
    each = PARTS * own_slots
    rows = groups * each
    expert = iota((rows, count), 0) // each * per_group + lax.axis_index("y")
    wide = iota((count, lanes), 1) % count
    at = iota((count, lanes), 0)
    ranker = jnp.where(at < wide, 1.0, jnp.where(at == wide, float(LATE), 0.0)).astype(BF16)
    row = iota((rows, lanes), 0) % each
    here = row // own_slots == iota((rows, lanes), 1) // count
    wanted = (row % own_slots + (LATE + own_slots * lax.axis_index("core"))).astype(F32)
    copies[0].wait()
    copies[1].wait()
    hit = jnp.zeros((rows, count), F32)
    score = jnp.zeros((rows, count), F32)
    for e in range(ids.shape[0]):
        same = ids[e : e + 1, :] == expert
        hit = jnp.where(same, 1.0, hit)
        score = jnp.where(same, scores[e : e + 1, :].astype(F32), score)
    rank = dot(hit.astype(BF16), ranker)
    found = rank == wanted
    mark = jnp.where(found & here, 1.0, 0.0).astype(BF16)
    slot_score = jnp.sum(jnp.where(found[:, :count], score, 0.0), axis=1, keepdims=True)
    part = tokens.shape[1] // PARTS
    copies[2].wait()
    out[:, :part] = dot(mark, stacked_parts(tokens)).astype(BF16)
    copies[3].wait()
    out[:, part:] = (slot_score * dot(mark, stacked_parts(grads))).astype(BF16)


ENTRIES = ((0, 0), (0, 1), (0, 2), (1, 2), (1, 3), (1, 4))
PIECE = 16


def describe(groups, per_group, slots, pad, ids, gather, place, order):
    ids_now = ids[...]
    tokens = ids_now.shape[1]
    experts = groups * per_group
    hit = picked(ids_now, iota((experts, tokens), 0)) > 0.5
    rank = dot(hit.astype(BF16), before(tokens, tokens))
    code = jnp.where(hit, rank, -1.0).astype(BF16)
    lanes = experts * PIECE
    widen = (iota((experts, lanes), 1) // PIECE == iota((experts, lanes), 0)).astype(BF16)
    spread = dot_first(code, widen).astype(jnp.int32)
    row = iota((tokens, lanes), 1) % PIECE
    for n, (odd, part) in enumerate(ENTRIES):
        mark = (spread == 2 * (row % 3) + odd) & (row // 3 == part)
        gather[n * tokens : (n + 1) * tokens, :] = mark.astype(BF16)

    own_slots = slots // CORES
    rows = groups * own_slots
    at, col = iota(place.shape, 0), iota(place.shape, 1)
    tall = place.shape[1] // (len(ENTRIES) * CORES)
    row, source = at % PIECE, col % tall
    slot = source % own_slots + col // tall % CORES * own_slots
    mark = jnp.zeros(place.shape, jnp.bool_)
    for n, (odd, part) in enumerate(ENTRIES):
        mark |= (col // (CORES * tall) == n) & (row // 3 == part) & (slot == 2 * (row % 3) + odd)
    place[...] = (mark & (at // PIECE == source // own_slots) & (source < rows)).astype(BF16)

    at = iota(order.shape[1:], 0)
    inner = at % pad
    source = inner // own_slots * (PARTS * own_slots) + at // pad * own_slots + inner % own_slots
    for h in range(2):
        here = iota(order.shape[1:], 1) + h * order.shape[2]
        order[h] = ((source == here) & (inner < rows)).astype(BF16)


def round_up(n, k):
    return -(-n // k) * k


def backward(homes, order, parts, pair, pair_far, down, down_far, write, ins, grads):
    blocks = len(homes)
    pad, part = ins.shape[1] // blocks, ins.shape[2]
    for k in range(blocks):
        moved = dot(order[0], parts[2 * k]) + dot(order[1], parts[2 * k + 1])
        moved = moved.astype(BF16)
        for f in range(PARTS):
            at = slice(f * pad, (f + 1) * pad)
            ins[f, k * pad : (k + 1) * pad, :] = moved[at, :part]
            grads[f, k * pad : (k + 1) * pad, :] = moved[at, part:]
    hidden = down.shape[0]
    count = blocks * pad
    pre = [jnp.zeros((count, 2 * hidden), F32) for _ in range(2)]
    act = [jnp.zeros((count, hidden), F32) for _ in range(2)]
    for f in range(PARTS):
        lanes = slice(f * part, (f + 1) * part)
        for s, weight in enumerate((pair, pair_far)):
            pre[s] += dot_last(ins[f], weight[:, lanes])
        for s, weight in enumerate((down, down_far)):
            act[s] += dot_last(grads[f], weight[:, lanes])
    hid = []
    for s in range(2):
        gate, up = pre[s][:, :hidden], pre[s][:, hidden:]
        sig = jax.nn.sigmoid(gate)
        gate_grad = act[s] * up * sig * (1.0 + gate * (1.0 - sig))
        up_grad = act[s] * gate * sig
        hid.append(jnp.concatenate([gate_grad, up_grad], axis=1).astype(BF16))
    low = iota((count, LANES), 1) < LANES // 2

    def join(left, right):
        return jnp.where(low, left, right)

    def turn(x):
        return pltpu.roll(x, LANES // 2, 1)

    for f in range(pair.shape[1] // (10 * LANES)):
        tiles = []
        for y in (2 * f, 2 * f + 1):
            lanes = slice(5 * LANES * y, 5 * LANES * (y + 1))
            total = dot(hid[0], pair[:, lanes]) + dot(hid[1], pair_far[:, lanes])
            tiles.append([total[:, t * LANES : (t + 1) * LANES] for t in range(5)])
        a, b = tiles
        at = [turn(a[t]) for t in (2, 3, 4)]
        bt = [turn(b[t]) for t in (0, 1, 2)]
        first = [a[0], a[1], join(a[2], bt[0]), join(bt[0], bt[1]), join(bt[1], bt[2])]
        second = [join(at[0], at[1]), join(at[1], at[2]), join(at[2], b[2]), b[3], b[4]]
        for core, group in enumerate((first, second)):
            for t, tile in enumerate(group):
                for k, home in enumerate(homes):
                    write(home, core, 5 * f + t, tile[k * pad : (k + 1) * pad])


def home_of(shift, members):
    return lax.rem(lax.axis_index("member") + shift, members)


def backward_near(members, tall, order, near, *refs):
    parts, (pair, pair_far, down, down_far, out, ins, grads) = refs[:-7], refs[-7:]
    middle = order.shape[2]
    halves = [near[:middle, :], near[middle:, :]] + [p[...] for p in parts]

    def write(home, core, t, rows):
        out[home * CORES + core, t * tall : (t + 1) * tall, :] = rows[:tall].astype(BF16)

    homes = [home_of(shift, members) for shift in (0, members - 1, 1)]
    backward(homes, order, halves, pair, pair_far, down, down_far, write, ins, grads)


def backward_opposite(members, tall, order, top, bottom, pair, pair_far, down, down_far, before_out, out, ins, grads, held, done):
    del before_out

    def write(home, core, t, rows):
        held[core, t * tall : (t + 1) * tall, :] = rows[:tall].astype(BF16)

    halves = [top[...], bottom[...]]
    backward([None], order, halves, pair, pair_far, down, down_far, write, ins, grads)
    home = home_of(members // 2, members)
    copies = [
        pltpu.make_async_copy(held.at[core], out.at[home * CORES + core], done.at[core])
        for core in range(CORES)
    ]
    for copy in copies:
        copy.start()
    for copy in copies:
        copy.wait()


def total_pieces(groups, columns, tall, place, x, out):
    low = iota((tall, LANES), 1) < LANES // 2
    members = x.shape[0] // CORES
    for y in range(columns):
        sorted_entries = [[] for _ in ENTRIES]
        for c in range(CORES):
            tiles, turned = [], []
            for t in range(3):
                at = (5 * y // 2 + t) * tall
                tile = x[c, at : at + tall, :].astype(F32)
                for m in range(1, members):
                    tile += x[m * CORES + c, at : at + tall, :].astype(F32)
                tiles.append(tile)
                turned.append(pltpu.roll(tile, LANES // 2, 1))
            first = [
                jnp.where(low, turned[0], turned[1]),
                jnp.where(low, turned[1], turned[2]),
            ]
            if y % 2 == 0:
                seam = [jnp.where(low, tiles[2], 0.0), jnp.where(low, 0.0, turned[0])]
                entries = tiles[:2] + seam + first
            else:
                seam = [jnp.where(low, turned[2], 0.0), jnp.where(low, 0.0, tiles[0])]
                entries = first + seam + tiles[1:]
            for n, entry in enumerate(entries):
                sorted_entries[n].append(entry)
        stack = jnp.concatenate([e for pair in sorted_entries for e in pair], axis=0)
        moved = dot(place[...], stack.astype(BF16)).astype(BF16)
        for g in range(groups):
            out[g * columns + y] = moved[g * PIECE : (g + 1) * PIECE]


def finish(gather, x, out):
    tokens, chunk = out.shape
    found = dot(gather[...], x[...])
    part = [found[n * tokens : (n + 1) * tokens] for n in range(len(ENTRIES))]
    turned = [pltpu.roll(p, LANES // 2, 1) for p in part[3:]]
    low = iota((tokens, LANES), 1) < LANES // 2
    out[:, :LANES] = (part[0] + jnp.where(low, turned[0], turned[1])).astype(BF16)
    out[:, LANES : 2 * LANES] = (part[1] + jnp.where(low, turned[1], turned[2])).astype(BF16)
    last = (part[2] + turned[2]).astype(BF16)
    out[:, 2 * LANES :] = last[:, : chunk - 2 * LANES]


def per_device(tokens_in, out_grad, scores, expert_ids, w_in, w_down):
    groups, members = lax.axis_size("group"), lax.axis_size("member")
    columns = lax.axis_size("y")
    tokens, width = tokens_in.shape
    picks = expert_ids.shape[1]
    pairs = picks // TGROUPS
    slots = pairs * (TGROUPS * tokens // groups) // columns
    part = width // PARTS
    chunk = width // (CORES * columns)
    hidden = w_down.shape[1]
    block_rows = groups * slots // CORES
    pad, tall = round_up(block_rows, 16), round_up(block_rows, 8)
    packed_rows = block_rows * PARTS
    middle = packed_rows // 2

    def struct(shape, kind):
        return jax.ShapeDtypeStruct(shape, kind)

    def exchange(x, axis):
        return lax.all_to_all(x, axis, split_axis=0, concat_axis=0, tiled=True)

    def up(x):
        return lax.ppermute(x, "member", [(i, (i + 1) % members) for i in range(members)])

    def down(x):
        return lax.ppermute(x, "member", [(i, (i - 1) % members) for i in range(members)])

    def far(x):
        return lax.ppermute(x, "core", [(0, 1), (1, 0)])

    def bind(body, *front):
        return lambda *refs: body(*front, *refs)

    ids = expert_ids.T
    sent = call(
        bind(pack, groups, columns, slots),
        struct((packed_rows, 2 * part), BF16),
        ids, scores.T, tokens_in, out_grad,
        far={i: pltpu.HBM for i in range(4)}, room=60,
        scratch=(
            pltpu.VMEM(ids.shape, ids.dtype),
            pltpu.VMEM(ids.shape, BF16),
            pltpu.VMEM((tokens, width), BF16),
            pltpu.VMEM((tokens, width), BF16),
            pltpu.SemaphoreType.DMA((4,)),
        ),
    )
    w_pair = w_in[0].reshape(2 * hidden, width)
    w_out = w_down[0]
    sent, ids, pair_late, out_late = lax.optimization_barrier((sent, ids, w_pair, w_out))
    near = exchange(sent.reshape(groups, -1, 2 * part), "group").reshape(sent.shape)
    pair_far, out_far = far(pair_late), far(out_late)
    gather, place, order = call(
        bind(describe, groups, columns, slots, pad),
        (
            struct((len(ENTRIES) * tokens, groups * columns * PIECE), BF16),
            struct((groups * PIECE, len(ENTRIES) * CORES * tall), BF16),
            struct((2, PARTS * pad, middle), BF16),
        ),
        ids,
    )
    near, order, pair_far, out_far = lax.optimization_barrier((near, order, pair_far, out_far))
    weights = (w_pair, pair_far, w_out, out_far)

    top, bottom = near[:middle], near[middle:]
    below_top, above_bottom = up(top), down(bottom)
    below_bottom, above_top = up(bottom), down(top)
    opposite = (up(below_top), down(above_bottom))

    lane_tiles = width // (CORES * LANES)
    result = struct((members * CORES, lane_tiles * tall, LANES), BF16)

    def rows(blocks):
        return pltpu.VMEM((PARTS, blocks * pad, part), BF16)

    partial = call(
        bind(backward_near, members, tall),
        result,
        order, near, below_top, below_bottom, above_top, above_bottom, *weights,
        flops=2 * 3 * pad * width * 10 * hidden, scratch=(rows(3), rows(3)),
    )
    partial = call(
        bind(backward_opposite, members, tall),
        result,
        order, *opposite, *weights, partial,
        far={7: pl.ANY}, far_out=True, alias=7,
        flops=2 * pad * width * 10 * hidden,
        scratch=(
            rows(1),
            rows(1),
            pltpu.VMEM((CORES,) + result.shape[1:], BF16),
            pltpu.SemaphoreType.DMA((CORES,)),
        ),
    )
    pieces = call(
        bind(total_pieces, groups, columns, tall),
        struct((groups * columns, PIECE, LANES), BF16),
        place, exchange(partial, ("member", "core")),
    )
    arrived = exchange(pieces, ("group", "y")).reshape(-1, LANES)
    return call(finish, struct((tokens, chunk), BF16), gather, arrived)


def solution(mesh):
    shape = mesh.devices.shape
    split = Mesh(
        mesh.devices.reshape(shape[0], shape[1], shape[2] // 2, 2),
        ("group", "member", "y", "core"),
    )
    in_specs = (
        P(("group", "member"), None),
        P(("group", "member"), None),
        P(("group", "member"), None),
        P(("group", "member"), None),
        P(("group", "y", "core"), None, "member", None),
        P(("group", "y", "core"), "member", None),
    )
    out_specs = P(("group", "member"), ("y", "core"))
    return jax.shard_map(
        per_device, mesh=split, in_specs=in_specs, out_specs=out_specs, check_vma=False
    )
```

```python
from types import MappingProxyType

import jax
import jax.numpy as jnp
from jax import lax
from jax.experimental import pallas as pl
from jax.experimental.pallas import tpu as pltpu
from jax.sharding import Mesh, PartitionSpec as P

TGROUPS = 3
PARTS = 8
CORES = 2
LATE = 128
LANES = 128
INTERPRET = False
F32 = jnp.float32
BF16 = jnp.bfloat16


def iota(shape, dim):
    return lax.broadcasted_iota(jnp.int32, shape, dim)


def call(body, out_shape, *args, scratch=(), far=MappingProxyType({}), far_out=False, alias=None, flops=0, room=20):
    moved = sum(a.size * a.dtype.itemsize for a in args)
    target = pl.ANY if far_out else pltpu.VMEM
    return pl.pallas_call(
        body,
        out_shape=out_shape,
        in_specs=[pl.BlockSpec(memory_space=far.get(i, pltpu.VMEM)) for i in range(len(args))],
        out_specs=jax.tree.map(lambda s: pl.BlockSpec(memory_space=target), out_shape),
        scratch_shapes=list(scratch),
        input_output_aliases={} if alias is None else {alias: 0},
        compiler_params=pltpu.CompilerParams(vmem_limit_bytes=room * 1024 * 1024),
        cost_estimate=pl.CostEstimate(flops=flops, bytes_accessed=moved, transcendentals=0),
        interpret=INTERPRET,
    )(*args)


def dot(a, b):
    return jnp.dot(a, b, preferred_element_type=F32)


def dot_last(a, b):
    return lax.dot_general(a, b, (((1,), (1,)), ((), ())), preferred_element_type=F32)


def dot_first(a, b):
    return lax.dot_general(a, b, (((0,), (0,)), ((), ())), preferred_element_type=F32)


def picked(ids, target):
    hit = jnp.zeros(target.shape, F32)
    for e in range(ids.shape[0]):
        hit += (ids[e : e + 1, :] == target).astype(F32)
    return hit


def before(tokens, lanes):
    return (iota((tokens, lanes), 0) < iota((tokens, lanes), 1) % tokens).astype(BF16)


def stacked_parts(ref):
    part = ref.shape[1] // PARTS
    return jnp.concatenate([ref[:, f * part : (f + 1) * part] for f in range(PARTS)], axis=0)


def pack(groups, per_group, slots, ids_far, scores_far, tokens_far, grads_far, out, ids, scores, tokens, grads, done):
    sources, targets = (ids_far, scores_far, tokens_far, grads_far), (ids, scores, tokens, grads)
    copies = [
        pltpu.make_async_copy(source, target, done.at[n])
        for n, (source, target) in enumerate(zip(sources, targets))
    ]
    for copy in copies:
        copy.start()
    count = ids.shape[1]
    lanes = PARTS * count
    own_slots = slots // CORES
    each = PARTS * own_slots
    rows = groups * each
    expert = iota((rows, count), 0) // each * per_group + lax.axis_index("y")
    wide = iota((count, lanes), 1) % count
    at = iota((count, lanes), 0)
    ranker = jnp.where(at < wide, 1.0, jnp.where(at == wide, float(LATE), 0.0)).astype(BF16)
    row = iota((rows, lanes), 0) % each
    here = row // own_slots == iota((rows, lanes), 1) // count
    wanted = (row % own_slots + (LATE + own_slots * lax.axis_index("core"))).astype(F32)
    copies[0].wait()
    copies[1].wait()
    hit = jnp.zeros((rows, count), F32)
    score = jnp.zeros((rows, count), F32)
    for e in range(ids.shape[0]):
        same = ids[e : e + 1, :] == expert
        hit = jnp.where(same, 1.0, hit)
        score = jnp.where(same, scores[e : e + 1, :].astype(F32), score)
    rank = dot(hit.astype(BF16), ranker)
    found = rank == wanted
    mark = jnp.where(found & here, 1.0, 0.0).astype(BF16)
    slot_score = jnp.sum(jnp.where(found[:, :count], score, 0.0), axis=1, keepdims=True)
    part = tokens.shape[1] // PARTS
    copies[2].wait()
    out[:, :part] = dot(mark, stacked_parts(tokens)).astype(BF16)
    copies[3].wait()
    out[:, part:] = (slot_score * dot(mark, stacked_parts(grads))).astype(BF16)


ENTRIES = ((0, 0), (0, 1), (0, 2), (1, 2), (1, 3), (1, 4))
PIECE = 16


def describe(groups, per_group, slots, ids, gather, place, order):
    ids_now = ids[...]
    tokens = ids_now.shape[1]
    experts = groups * per_group
    hit = picked(ids_now, iota((experts, tokens), 0)) > 0.5
    rank = dot(hit.astype(BF16), before(tokens, tokens))
    code = jnp.where(hit, rank, -1.0).astype(BF16)
    lanes = experts * PIECE
    widen = (iota((experts, lanes), 1) // PIECE == iota((experts, lanes), 0)).astype(BF16)
    spread = dot_first(code, widen).astype(jnp.int32)
    row = iota((tokens, lanes), 1) % PIECE
    for n, (odd, part) in enumerate(ENTRIES):
        mark = (spread == 2 * (row % 3) + odd) & (row // 3 == part)
        gather[n * tokens : (n + 1) * tokens, :] = mark.astype(BF16)

    own_slots = slots // CORES
    rows = groups * own_slots
    at, col = iota(place.shape, 0), iota(place.shape, 1)
    tall = place.shape[1] // (len(ENTRIES) * CORES)
    row, source = at % PIECE, col % tall
    slot = source % own_slots + col // tall % CORES * own_slots
    mark = jnp.zeros(place.shape, jnp.bool_)
    for n, (odd, part) in enumerate(ENTRIES):
        mark |= (col // (CORES * tall) == n) & (row // 3 == part) & (slot == 2 * (row % 3) + odd)
    place[...] = (mark & (at // PIECE == source // own_slots) & (source < rows)).astype(BF16)

    span = order.shape[1] // PARTS
    at, here = iota(order.shape[1:], 0), iota(order.shape[1:], 1)
    for h in range(2):
        inner = at % span + h * (tall - span - rows // 2)
        source = inner // own_slots * (PARTS * own_slots) + at // span * own_slots + inner % own_slots
        order[h] = ((source == here) & (inner >= 0) & (inner < rows // 2)).astype(BF16)


def round_up(n, k):
    return -(-n // k) * k


def backward(homes, tall, order, halves, ready, pairs, downs, write, ins, grads):
    span = order.shape[1] // PARTS
    apart = tall - span
    wide = ins.shape[2]
    part = wide // 2
    for k in range(len(homes)):
        a, b = dot(order[0], halves[2 * k]), dot(order[1], halves[2 * k + 1])
        for f in range(PARTS):
            at = f * span
            seam = a[at + apart : at + span] + b[at : at + span - apart]
            block = [a[at : at + apart], seam, b[at + span - apart : at + span]]
            block = jnp.concatenate(block, axis=0).astype(BF16)
            rows, lanes = slice(k * tall, (k + 1) * tall), slice(f % 2 * part, (f % 2 + 1) * part)
            ins[f // 2, rows, lanes] = block[:, :part]
            grads[f // 2, rows, lanes] = block[:, part:]
    for copy in ready:
        copy.wait()
    hidden = downs.shape[0] // CORES
    count = ins.shape[1]
    pre = jnp.zeros((2 * CORES * hidden, count), F32)
    act = jnp.zeros((CORES * hidden, count), F32)
    for f in range(PARTS // 2):
        lanes = slice(f * wide, (f + 1) * wide)
        pre += dot_last(pairs[:, lanes], ins[f])
        act += dot_last(downs[:, lanes], grads[f])
    parts = []
    for s in range(CORES):
        gate, up = pre[2 * s * hidden :][:hidden], pre[(2 * s + 1) * hidden :][:hidden]
        slope = act[s * hidden :][:hidden]
        sig = jax.nn.sigmoid(gate)
        parts.append(slope * up * sig * (1.0 + gate * (1.0 - sig)))
        parts.append(slope * gate * sig)
    hid = jnp.concatenate(parts, axis=0).T.astype(BF16)
    low = iota((count, LANES), 1) < LANES // 2

    def join(left, right):
        return jnp.where(low, left, right)

    def turn(x):
        return pltpu.roll(x, LANES // 2, 1)

    for f in range(pairs.shape[1] // (10 * LANES)):
        tiles = []
        for y in (2 * f, 2 * f + 1):
            lanes = slice(5 * LANES * y, 5 * LANES * (y + 1))
            total = dot(hid, pairs[:, lanes])
            tiles.append([total[:, t * LANES : (t + 1) * LANES] for t in range(5)])
        a, b = tiles
        at = [turn(a[t]) for t in (2, 3, 4)]
        bt = [turn(b[t]) for t in (0, 1, 2)]
        first = [a[0], a[1], join(a[2], bt[0]), join(bt[0], bt[1]), join(bt[1], bt[2])]
        second = [join(at[0], at[1]), join(at[1], at[2]), join(at[2], b[2]), b[3], b[4]]
        for core, group in enumerate((first, second)):
            for t, tile in enumerate(group):
                for k, home in enumerate(homes):
                    write(home, core, 5 * f + t, tile[k * tall : (k + 1) * tall])


def home_of(shift, members):
    return lax.rem(lax.axis_index("member") + shift, members)


def backward_near(members, tall, order, near, *refs):
    parts, weights, (out, pairs, downs, ins, grads, done) = refs[:4], refs[4:8], refs[8:]
    deep, flat = pairs.shape[0] // CORES, downs.shape[0] // CORES
    targets = (pairs.at[:deep], pairs.at[deep:], downs.at[:flat], downs.at[flat:])
    copies = [
        pltpu.make_async_copy(source, target, done.at[n])
        for n, (source, target) in enumerate(zip(weights, targets))
    ]
    for copy in copies:
        copy.start()
    middle = order.shape[2]
    halves = [near[:middle, :], near[middle:, :]] + [p[...] for p in parts]

    def write(home, core, t, rows):
        out[home * CORES + core, t * tall : (t + 1) * tall, :] = rows.astype(BF16)

    homes = [home_of(shift, members) for shift in (0, members - 1, 1)]
    backward(homes, tall, order, halves, copies, pairs, downs, write, ins, grads)


def backward_opposite(members, tall, order, top, bottom, pairs, downs, *refs):
    out, ins, grads, held, sent = refs[1:]
    home = home_of(members // 2, members)
    copies = []

    def write(_, core, t, rows):
        held[core, t * tall : (t + 1) * tall, :] = rows.astype(BF16)
        if t % 5 == 4:
            at = pl.ds((t - 4) * tall, 5 * tall)
            copy = pltpu.make_async_copy(
                held.at[core, at], out.at[home * CORES + core, at], sent.at[core, t // 5]
            )
            copy.start()
            copies.append(copy)

    halves = [top[...], bottom[...]]
    backward([home], tall, order, halves, [], pairs, downs, write, ins, grads)
    for copy in copies:
        copy.wait()


def total_pieces(groups, columns, tall, place, x, out):
    low = iota((tall, LANES), 1) < LANES // 2
    members = x.shape[0] // CORES
    for y in range(columns):
        sorted_entries = [[] for _ in ENTRIES]
        for c in range(CORES):
            tiles, turned = [], []
            for t in range(3):
                at = (5 * y // 2 + t) * tall
                tile = x[c, at : at + tall, :].astype(F32)
                for m in range(1, members):
                    tile += x[m * CORES + c, at : at + tall, :].astype(F32)
                tiles.append(tile)
                turned.append(pltpu.roll(tile, LANES // 2, 1))
            first = [
                jnp.where(low, turned[0], turned[1]),
                jnp.where(low, turned[1], turned[2]),
            ]
            if y % 2 == 0:
                seam = [jnp.where(low, tiles[2], 0.0), jnp.where(low, 0.0, turned[0])]
                entries = tiles[:2] + seam + first
            else:
                seam = [jnp.where(low, turned[2], 0.0), jnp.where(low, 0.0, tiles[0])]
                entries = first + seam + tiles[1:]
            for n, entry in enumerate(entries):
                sorted_entries[n].append(entry)
        stack = jnp.concatenate([e for pair in sorted_entries for e in pair], axis=0)
        moved = dot(place[...], stack.astype(BF16)).astype(BF16)
        for g in range(groups):
            out[g * columns + y] = moved[g * PIECE : (g + 1) * PIECE]


def finish(gather, x, out):
    tokens, chunk = out.shape
    found = dot(gather[...], x[...])
    part = [found[n * tokens : (n + 1) * tokens] for n in range(len(ENTRIES))]
    turned = [pltpu.roll(p, LANES // 2, 1) for p in part[3:]]
    low = iota((tokens, LANES), 1) < LANES // 2
    out[:, :LANES] = (part[0] + jnp.where(low, turned[0], turned[1])).astype(BF16)
    out[:, LANES : 2 * LANES] = (part[1] + jnp.where(low, turned[1], turned[2])).astype(BF16)
    last = (part[2] + turned[2]).astype(BF16)
    out[:, 2 * LANES :] = last[:, : chunk - 2 * LANES]


def per_device(tokens_in, out_grad, scores, expert_ids, w_in, w_down):
    groups, members = lax.axis_size("group"), lax.axis_size("member")
    columns = lax.axis_size("y")
    tokens, width = tokens_in.shape
    picks = expert_ids.shape[1]
    pairs = picks // TGROUPS
    slots = pairs * (TGROUPS * tokens // groups) // columns
    part = width // PARTS
    chunk = width // (CORES * columns)
    hidden = w_down.shape[1]
    block_rows = groups * slots // CORES
    tall, span = round_up(block_rows, 8), round_up(block_rows // 2, 8)
    packed_rows = block_rows * PARTS
    middle = packed_rows // 2

    def struct(shape, kind):
        return jax.ShapeDtypeStruct(shape, kind)

    def exchange(x, axis):
        return lax.all_to_all(x, axis, split_axis=0, concat_axis=0, tiled=True)

    def up(x):
        return lax.ppermute(x, "member", [(i, (i + 1) % members) for i in range(members)])

    def down(x):
        return lax.ppermute(x, "member", [(i, (i - 1) % members) for i in range(members)])

    def far(x):
        return lax.ppermute(x, "core", [(0, 1), (1, 0)])

    def bind(body, *front):
        return lambda *refs: body(*front, *refs)

    ids = expert_ids.T
    sent = call(
        bind(pack, groups, columns, slots),
        struct((packed_rows, 2 * part), BF16),
        ids, scores.T, tokens_in, out_grad,
        far={i: pltpu.HBM for i in range(4)}, room=60,
        scratch=(
            pltpu.VMEM(ids.shape, ids.dtype),
            pltpu.VMEM(ids.shape, BF16),
            pltpu.VMEM((tokens, width), BF16),
            pltpu.VMEM((tokens, width), BF16),
            pltpu.SemaphoreType.DMA((4,)),
        ),
    )
    w_pair = w_in[0].reshape(2 * hidden, width)
    w_out = w_down[0]
    sent, ids, pair_late, out_late = lax.optimization_barrier((sent, ids, w_pair, w_out))
    near = exchange(sent.reshape(groups, -1, 2 * part), "group").reshape(sent.shape)
    pair_far, out_far = far(pair_late), far(out_late)
    gather, place, order = call(
        bind(describe, groups, columns, slots),
        (
            struct((len(ENTRIES) * tokens, groups * columns * PIECE), BF16),
            struct((groups * PIECE, len(ENTRIES) * CORES * tall), BF16),
            struct((2, PARTS * span, middle), BF16),
        ),
        ids,
    )
    near, order = lax.optimization_barrier((near, order))
    weights = (w_pair, pair_far, w_out, out_far)

    top, bottom = near[:middle], near[middle:]
    below_top, above_bottom = up(top), down(bottom)
    below_bottom = up(bottom)
    above_top = down(top)
    opposite = (up(below_top), down(above_bottom))

    lane_tiles = width // (CORES * LANES)
    result = struct((members * CORES, lane_tiles * tall, LANES), BF16)

    def rows(blocks):
        return pltpu.VMEM((PARTS // 2, blocks * tall, 2 * part), BF16)

    partial, pairs_all, downs_all = call(
        bind(backward_near, members, tall),
        (
            result,
            struct((CORES * 2 * hidden, width), BF16),
            struct((CORES * hidden, width), BF16),
        ),
        order, near, below_top, below_bottom, above_top, above_bottom, *weights,
        far={6: pl.ANY, 7: pltpu.HBM, 8: pl.ANY, 9: pltpu.HBM},
        flops=2 * 3 * tall * width * 10 * hidden,
        scratch=(rows(3), rows(3), pltpu.SemaphoreType.DMA((4,))),
    )
    partial = call(
        bind(backward_opposite, members, tall),
        result,
        order, *opposite, pairs_all, downs_all, partial,
        far={5: pl.ANY}, far_out=True, alias=5,
        flops=2 * tall * width * 10 * hidden,
        scratch=(
            rows(1),
            rows(1),
            pltpu.VMEM((CORES,) + result.shape[1:], BF16),
            pltpu.SemaphoreType.DMA((CORES, lane_tiles // 5)),
        ),
    )
    pieces = call(
        bind(total_pieces, groups, columns, tall),
        struct((groups * columns, PIECE, LANES), BF16),
        place, exchange(partial, ("member", "core")),
    )
    arrived = exchange(pieces, ("group", "y")).reshape(-1, LANES)
    return call(finish, struct((tokens, chunk), BF16), gather, arrived)


def solution(mesh):
    shape = mesh.devices.shape
    split = Mesh(
        mesh.devices.reshape(shape[0], shape[1], shape[2] // 2, 2),
        ("group", "member", "y", "core"),
    )
    in_specs = (
        P(("group", "member"), None),
        P(("group", "member"), None),
        P(("group", "member"), None),
        P(("group", "member"), None),
        P(("group", "y", "core"), None, "member", None),
        P(("group", "y", "core"), "member", None),
    )
    out_specs = P(("group", "member"), ("y", "core"))
    return jax.shard_map(
        per_device, mesh=split, in_specs=in_specs, out_specs=out_specs, check_vma=False
    )
```

```python
from types import MappingProxyType

import jax
import jax.numpy as jnp
from jax import lax
from jax.experimental import pallas as pl
from jax.experimental.pallas import tpu as pltpu
from jax.sharding import Mesh, PartitionSpec as P

TGROUPS = 3
PARTS = 8
CORES = 2
LATE = 128
LANES = 128
INTERPRET = False
F32 = jnp.float32
BF16 = jnp.bfloat16


def iota(shape, dim):
    return lax.broadcasted_iota(jnp.int32, shape, dim)


def call(body, out_shape, *args, scratch=(), far=MappingProxyType({}), far_out=False, alias=None, flops=0, room=20):
    moved = sum(a.size * a.dtype.itemsize for a in args)
    target = pl.ANY if far_out else pltpu.VMEM
    return pl.pallas_call(
        body,
        out_shape=out_shape,
        in_specs=[pl.BlockSpec(memory_space=far.get(i, pltpu.VMEM)) for i in range(len(args))],
        out_specs=jax.tree.map(lambda s: pl.BlockSpec(memory_space=target), out_shape),
        scratch_shapes=list(scratch),
        input_output_aliases={} if alias is None else {alias: 0},
        compiler_params=pltpu.CompilerParams(vmem_limit_bytes=room * 1024 * 1024),
        cost_estimate=pl.CostEstimate(flops=flops, bytes_accessed=moved, transcendentals=0),
        interpret=INTERPRET,
    )(*args)


def dot(a, b):
    return jnp.dot(a, b, preferred_element_type=F32)


def dot_last(a, b):
    return lax.dot_general(a, b, (((1,), (1,)), ((), ())), preferred_element_type=F32)


def dot_first(a, b):
    return lax.dot_general(a, b, (((0,), (0,)), ((), ())), preferred_element_type=F32)


def picked(ids, target):
    hit = jnp.zeros(target.shape, F32)
    for e in range(ids.shape[0]):
        hit += (ids[e : e + 1, :] == target).astype(F32)
    return hit


def before(tokens, lanes):
    return (iota((tokens, lanes), 0) < iota((tokens, lanes), 1) % tokens).astype(BF16)


def stacked_parts(ref):
    part = ref.shape[1] // PARTS
    return jnp.concatenate([ref[:, f * part : (f + 1) * part] for f in range(PARTS)], axis=0)


def pack(groups, per_group, slots, ids_far, scores_far, tokens_far, grads_far, out, ids, scores, tokens, grads, done):
    sources, targets = (ids_far, scores_far, tokens_far, grads_far), (ids, scores, tokens, grads)
    copies = [
        pltpu.make_async_copy(source, target, done.at[n])
        for n, (source, target) in enumerate(zip(sources, targets))
    ]
    for copy in copies:
        copy.start()
    count = ids.shape[1]
    lanes = PARTS * count
    own_slots = slots // CORES
    each = PARTS * own_slots
    rows = groups * each
    expert = iota((rows, count), 0) // each * per_group + lax.axis_index("y")
    wide = iota((count, lanes), 1) % count
    at = iota((count, lanes), 0)
    ranker = jnp.where(at < wide, 1.0, jnp.where(at == wide, float(LATE), 0.0)).astype(BF16)
    row = iota((rows, lanes), 0) % each
    here = row // own_slots == iota((rows, lanes), 1) // count
    wanted = (row % own_slots + (LATE + own_slots * lax.axis_index("core"))).astype(F32)
    copies[0].wait()
    copies[1].wait()
    hit = jnp.zeros((rows, count), F32)
    score = jnp.zeros((rows, count), F32)
    for e in range(ids.shape[0]):
        same = ids[e : e + 1, :] == expert
        hit = jnp.where(same, 1.0, hit)
        score = jnp.where(same, scores[e : e + 1, :].astype(F32), score)
    rank = dot(hit.astype(BF16), ranker)
    found = rank == wanted
    mark = jnp.where(found & here, 1.0, 0.0).astype(BF16)
    slot_score = jnp.sum(jnp.where(found[:, :count], score, 0.0), axis=1, keepdims=True)
    part = tokens.shape[1] // PARTS
    copies[2].wait()
    out[:, :part] = dot(mark, stacked_parts(tokens)).astype(BF16)
    copies[3].wait()
    out[:, part:] = (slot_score * dot(mark, stacked_parts(grads))).astype(BF16)


ENTRIES = ((0, 0), (0, 1), (0, 2), (1, 2), (1, 3), (1, 4))
PIECE = 16


def describe(groups, per_group, slots, ids, gather, place, order):
    ids_now = ids[...]
    tokens = ids_now.shape[1]
    experts = groups * per_group
    hit = picked(ids_now, iota((experts, tokens), 0)) > 0.5
    rank = dot(hit.astype(BF16), before(tokens, tokens))
    code = jnp.where(hit, rank, -1.0).astype(BF16)
    lanes = experts * PIECE
    widen = (iota((experts, lanes), 1) // PIECE == iota((experts, lanes), 0)).astype(BF16)
    spread = dot_first(code, widen).astype(jnp.int32)
    row = iota((tokens, lanes), 1) % PIECE
    for n, (odd, part) in enumerate(ENTRIES):
        mark = (spread == 2 * (row % 3) + odd) & (row // 3 == part)
        gather[n * tokens : (n + 1) * tokens, :] = mark.astype(BF16)

    own_slots = slots // CORES
    rows = groups * own_slots
    at, col = iota(place.shape, 0), iota(place.shape, 1)
    tall = place.shape[1] // (len(ENTRIES) * CORES)
    row, source = at % PIECE, col % tall
    slot = source % own_slots + col // tall % CORES * own_slots
    mark = jnp.zeros(place.shape, jnp.bool_)
    for n, (odd, part) in enumerate(ENTRIES):
        mark |= (col // (CORES * tall) == n) & (row // 3 == part) & (slot == 2 * (row % 3) + odd)
    place[...] = (mark & (at // PIECE == source // own_slots) & (source < rows)).astype(BF16)

    span = order.shape[1] // PARTS
    at, here = iota(order.shape[1:], 0), iota(order.shape[1:], 1)
    for h in range(2):
        inner = at % span + h * (tall - span - rows // 2)
        source = inner // own_slots * (PARTS * own_slots) + at // span * own_slots + inner % own_slots
        order[h] = ((source == here) & (inner >= 0) & (inner < rows // 2)).astype(BF16)


def round_up(n, k):
    return -(-n // k) * k


def backward(homes, tall, order, halves, ready, pairs, downs, write, ins, grads):
    span = order.shape[1] // PARTS
    apart = tall - span
    wide = ins.shape[2]
    part = wide // 2
    for k in range(len(homes)):
        a, b = dot(order[0], halves[2 * k]), dot(order[1], halves[2 * k + 1])
        for f in range(PARTS):
            at = f * span
            seam = a[at + apart : at + span] + b[at : at + span - apart]
            block = [a[at : at + apart], seam, b[at + span - apart : at + span]]
            block = jnp.concatenate(block, axis=0).astype(BF16)
            rows, lanes = slice(k * tall, (k + 1) * tall), slice(f % 2 * part, (f % 2 + 1) * part)
            ins[f // 2, rows, lanes] = block[:, :part]
            grads[f // 2, rows, lanes] = block[:, part:]
    for copy in ready:
        copy.wait()
    hidden = downs.shape[0] // CORES
    count = ins.shape[1]
    pre = jnp.zeros((2 * CORES * hidden, count), F32)
    act = jnp.zeros((CORES * hidden, count), F32)
    for f in range(PARTS // 2):
        lanes = slice(f * wide, (f + 1) * wide)
        pre += dot_last(pairs[:, lanes], ins[f])
        act += dot_last(downs[:, lanes], grads[f])
    parts = []
    for s in range(CORES):
        gate, up = pre[2 * s * hidden :][:hidden], pre[(2 * s + 1) * hidden :][:hidden]
        slope = act[s * hidden :][:hidden]
        sig = jax.nn.sigmoid(gate)
        parts.append(slope * up * sig * (1.0 + gate * (1.0 - sig)))
        parts.append(slope * gate * sig)
    hid = jnp.concatenate(parts, axis=0).T.astype(BF16)
    low = iota((count, LANES), 1) < LANES // 2

    def join(left, right):
        return jnp.where(low, left, right)

    def turn(x):
        return pltpu.roll(x, LANES // 2, 1)

    for f in range(pairs.shape[1] // (10 * LANES)):
        tiles = []
        for y in (2 * f, 2 * f + 1):
            lanes = slice(5 * LANES * y, 5 * LANES * (y + 1))
            total = dot(hid, pairs[:, lanes])
            tiles.append([total[:, t * LANES : (t + 1) * LANES] for t in range(5)])
        a, b = tiles
        at = [turn(a[t]) for t in (2, 3, 4)]
        bt = [turn(b[t]) for t in (0, 1, 2)]
        first = [a[0], a[1], join(a[2], bt[0]), join(bt[0], bt[1]), join(bt[1], bt[2])]
        second = [join(at[0], at[1]), join(at[1], at[2]), join(at[2], b[2]), b[3], b[4]]
        for core, group in enumerate((first, second)):
            for t, tile in enumerate(group):
                for k, home in enumerate(homes):
                    write(home, core, 5 * f + t, tile[k * tall : (k + 1) * tall])


def home_of(shift, members):
    return lax.rem(lax.axis_index("member") + shift, members)


def paired(rows, store):
    held = {}

    def write(home, core, t, tile):
        if t % 2 == 0:
            held[id(home), core] = tile
            return
        first = held.pop((id(home), core))
        extra = 2 * (tile.shape[0] - rows)
        last = pltpu.roll(tile, tile.shape[0] - rows, 0)
        stop = tile.shape[0] - extra
        parts = (first[:stop], first[stop:] + last[:extra], last[extra:])
        begin = t // 2 * 2 * rows
        for part in parts:
            store(home, core, begin, part.astype(BF16))
            begin += part.shape[0]

    return write


def backward_near(members, tall, rows, order, near, *refs):
    parts, weights, (out, pairs, downs, ins, grads, done) = refs[:4], refs[4:8], refs[8:]
    deep, flat = pairs.shape[0] // CORES, downs.shape[0] // CORES
    targets = (pairs.at[:deep], pairs.at[deep:], downs.at[:flat], downs.at[flat:])
    copies = [
        pltpu.make_async_copy(source, target, done.at[n])
        for n, (source, target) in enumerate(zip(weights, targets))
    ]
    for copy in copies:
        copy.start()
    middle = order.shape[2]
    halves = [near[:middle, :], near[middle:, :]] + [p[...] for p in parts]

    def store(home, core, begin, part):
        out[home * CORES + core, begin : begin + part.shape[0], :] = part

    turn = (members - 2) * lax.axis_index("core")
    homes = [home_of(shift, members) for shift in (0, members - 1 - turn, 1 + turn)]
    backward(homes, tall, order, halves, copies, pairs, downs, paired(rows, store), ins, grads)


def backward_opposite(members, tall, rows, order, top, bottom, pairs, downs, *refs):
    out, ins, grads, held, sent = refs[1:]
    home = home_of(members // 2, members)
    chunk = held.shape[1] // sent.shape[1]
    copies = []

    def store(_, core, begin, part):
        end = begin + part.shape[0]
        held[core, begin:end, :] = part
        if end % chunk == 0:
            at = pl.ds(end - chunk, chunk)
            copy = pltpu.make_async_copy(
                held.at[core, at], out.at[home * CORES + core, at], sent.at[core, end // chunk - 1]
            )
            copy.start()
            copies.append(copy)

    halves = [top[...], bottom[...]]
    backward([home], tall, order, halves, [], pairs, downs, paired(rows, store), ins, grads)
    for copy in copies:
        copy.wait()


def total_pieces(groups, columns, tall, rows, place, x, out):
    low = iota((tall, LANES), 1) < LANES // 2
    members = x.shape[0] // CORES
    for y in range(columns):
        sorted_entries = [[] for _ in ENTRIES]
        for c in range(CORES):
            tiles, turned = [], []
            for t in range(3):
                number = 5 * y // 2 + t
                at = number // 2 * 2 * rows + number % 2 * (2 * rows - tall)
                tile = x[c, at : at + tall, :].astype(F32)
                for m in range(1, members):
                    tile += x[m * CORES + c, at : at + tall, :].astype(F32)
                if number % 2 == 1:
                    tile = pltpu.roll(tile, rows, 0)
                tiles.append(tile)
                turned.append(pltpu.roll(tile, LANES // 2, 1))
            first = [
                jnp.where(low, turned[0], turned[1]),
                jnp.where(low, turned[1], turned[2]),
            ]
            if y % 2 == 0:
                seam = [jnp.where(low, tiles[2], 0.0), jnp.where(low, 0.0, turned[0])]
                entries = tiles[:2] + seam + first
            else:
                seam = [jnp.where(low, turned[2], 0.0), jnp.where(low, 0.0, tiles[0])]
                entries = first + seam + tiles[1:]
            for n, entry in enumerate(entries):
                sorted_entries[n].append(entry)
        stack = jnp.concatenate([e for pair in sorted_entries for e in pair], axis=0)
        moved = dot(place[...], stack.astype(BF16)).astype(BF16)
        for g in range(groups):
            out[g * columns + y] = moved[g * PIECE : (g + 1) * PIECE]


def finish(gather, x, out):
    tokens, chunk = out.shape
    found = dot(gather[...], x[...])
    part = [found[n * tokens : (n + 1) * tokens] for n in range(len(ENTRIES))]
    turned = [pltpu.roll(p, LANES // 2, 1) for p in part[3:]]
    low = iota((tokens, LANES), 1) < LANES // 2
    out[:, :LANES] = (part[0] + jnp.where(low, turned[0], turned[1])).astype(BF16)
    out[:, LANES : 2 * LANES] = (part[1] + jnp.where(low, turned[1], turned[2])).astype(BF16)
    last = (part[2] + turned[2]).astype(BF16)
    out[:, 2 * LANES :] = last[:, : chunk - 2 * LANES]


def per_device(tokens_in, out_grad, scores, expert_ids, w_in, w_down):
    groups, members = lax.axis_size("group"), lax.axis_size("member")
    columns = lax.axis_size("y")
    tokens, width = tokens_in.shape
    picks = expert_ids.shape[1]
    pairs = picks // TGROUPS
    slots = pairs * (TGROUPS * tokens // groups) // columns
    part = width // PARTS
    chunk = width // (CORES * columns)
    hidden = w_down.shape[1]
    block_rows = groups * slots // CORES
    tall, span = round_up(block_rows, 8), round_up(block_rows // 2, 8)
    packed_rows = block_rows * PARTS
    middle = packed_rows // 2

    def struct(shape, kind):
        return jax.ShapeDtypeStruct(shape, kind)

    def exchange(x, axis):
        return lax.all_to_all(x, axis, split_axis=0, concat_axis=0, tiled=True)

    def shift(x, step):
        hops = [
            (CORES * i + c, CORES * ((i + step * (1 - 2 * c)) % members) + c)
            for i in range(members)
            for c in range(CORES)
        ]
        return lax.ppermute(x, ("member", "core"), hops)

    def up(x):
        return shift(x, 1)

    def down(x):
        return shift(x, -1)

    def far(x):
        return lax.ppermute(x, "core", [(0, 1), (1, 0)])

    def bind(body, *front):
        return lambda *refs: body(*front, *refs)

    ids = expert_ids.T
    sent = call(
        bind(pack, groups, columns, slots),
        struct((packed_rows, 2 * part), BF16),
        ids, scores.T, tokens_in, out_grad,
        far={i: pltpu.HBM for i in range(4)}, room=60,
        scratch=(
            pltpu.VMEM(ids.shape, ids.dtype),
            pltpu.VMEM(ids.shape, BF16),
            pltpu.VMEM((tokens, width), BF16),
            pltpu.VMEM((tokens, width), BF16),
            pltpu.SemaphoreType.DMA((4,)),
        ),
    )
    w_pair = w_in[0].reshape(2 * hidden, width)
    w_out = w_down[0]
    sent, ids, pair_late, out_late = lax.optimization_barrier((sent, ids, w_pair, w_out))
    near = exchange(sent.reshape(groups, -1, 2 * part), "group").reshape(sent.shape)
    pair_far, out_far = far(pair_late), far(out_late)
    gather, place, order = call(
        bind(describe, groups, columns, slots),
        (
            struct((len(ENTRIES) * tokens, groups * columns * PIECE), BF16),
            struct((groups * PIECE, len(ENTRIES) * CORES * tall), BF16),
            struct((2, PARTS * span, middle), BF16),
        ),
        ids,
    )
    near, order = lax.optimization_barrier((near, order))
    weights = (w_pair, pair_far, w_out, out_far)

    top, bottom = near[:middle], near[middle:]
    below_top, above_bottom = up(top), down(bottom)
    below_bottom = up(bottom)
    above_top = down(top)
    opposite = (up(below_top), down(above_bottom))

    lane_tiles = width // (CORES * LANES)
    result = struct((members * CORES, lane_tiles * block_rows, LANES), BF16)

    def rows(blocks):
        return pltpu.VMEM((PARTS // 2, blocks * tall, 2 * part), BF16)

    partial, pairs_all, downs_all = call(
        bind(backward_near, members, tall, block_rows),
        (
            result,
            struct((CORES * 2 * hidden, width), BF16),
            struct((CORES * hidden, width), BF16),
        ),
        order, near, below_top, below_bottom, above_top, above_bottom, *weights,
        far={6: pl.ANY, 7: pltpu.HBM, 8: pl.ANY, 9: pltpu.HBM},
        flops=2 * 3 * tall * width * 10 * hidden,
        scratch=(rows(3), rows(3), pltpu.SemaphoreType.DMA((4,))),
    )
    partial = call(
        bind(backward_opposite, members, tall, block_rows),
        result,
        order, *opposite, pairs_all, downs_all, partial,
        far={5: pl.ANY}, far_out=True, alias=5,
        flops=2 * tall * width * 10 * hidden,
        scratch=(
            rows(1),
            rows(1),
            pltpu.VMEM((CORES,) + result.shape[1:], BF16),
            pltpu.SemaphoreType.DMA((CORES, lane_tiles // 10)),
        ),
    )
    pieces = call(
        bind(total_pieces, groups, columns, tall, block_rows),
        struct((groups * columns, PIECE, LANES), BF16),
        place, exchange(partial, ("member", "core")),
    )
    arrived = exchange(pieces, ("group", "y")).reshape(-1, LANES)
    return call(finish, struct((tokens, chunk), BF16), gather, arrived)


def solution(mesh):
    shape = mesh.devices.shape
    split = Mesh(
        mesh.devices.reshape(shape[0], shape[1], shape[2] // 2, 2),
        ("group", "member", "y", "core"),
    )
    in_specs = (
        P(("group", "member"), None),
        P(("group", "member"), None),
        P(("group", "member"), None),
        P(("group", "member"), None),
        P(("group", "y", "core"), None, "member", None),
        P(("group", "y", "core"), "member", None),
    )
    out_specs = P(("group", "member"), ("y", "core"))
    return jax.shard_map(
        per_device, mesh=split, in_specs=in_specs, out_specs=out_specs, check_vma=False
    )
```

```python
from types import MappingProxyType

import jax
import jax.numpy as jnp
from jax import lax
from jax.experimental import pallas as pl
from jax.experimental.pallas import tpu as pltpu
from jax.sharding import Mesh, PartitionSpec as P

TGROUPS = 3
PARTS = 8
CORES = 2
LATE = 128
LANES = 128
INTERPRET = False
F32 = jnp.float32
BF16 = jnp.bfloat16


def iota(shape, dim):
    return lax.broadcasted_iota(jnp.int32, shape, dim)


def call(body, out_shape, *args, scratch=(), far=MappingProxyType({}), far_out=False, alias=None, flops=0, room=20):
    moved = sum(a.size * a.dtype.itemsize for a in args)
    target = pl.ANY if far_out else pltpu.VMEM
    return pl.pallas_call(
        body,
        out_shape=out_shape,
        in_specs=[pl.BlockSpec(memory_space=far.get(i, pltpu.VMEM)) for i in range(len(args))],
        out_specs=jax.tree.map(lambda s: pl.BlockSpec(memory_space=target), out_shape),
        scratch_shapes=list(scratch),
        input_output_aliases={} if alias is None else {alias: 0},
        compiler_params=pltpu.CompilerParams(vmem_limit_bytes=room * 1024 * 1024),
        cost_estimate=pl.CostEstimate(flops=flops, bytes_accessed=moved, transcendentals=0),
        interpret=INTERPRET,
    )(*args)


def dot(a, b):
    return jnp.dot(a, b, preferred_element_type=F32)


def dot_last(a, b):
    return lax.dot_general(a, b, (((1,), (1,)), ((), ())), preferred_element_type=F32)


def dot_first(a, b):
    return lax.dot_general(a, b, (((0,), (0,)), ((), ())), preferred_element_type=F32)


def picked(ids, target):
    hit = jnp.zeros(target.shape, F32)
    for e in range(ids.shape[0]):
        hit += (ids[e : e + 1, :] == target).astype(F32)
    return hit


def before(tokens, lanes):
    return (iota((tokens, lanes), 0) < iota((tokens, lanes), 1) % tokens).astype(BF16)


def stacked_parts(ref):
    part = ref.shape[1] // PARTS
    return jnp.concatenate([ref[:, f * part : (f + 1) * part] for f in range(PARTS)], axis=0)


def pack(groups, per_group, slots, ids_far, scores_far, tokens_far, grads_far, out, ids, scores, tokens, grads, done):
    sources, targets = (ids_far, scores_far, tokens_far, grads_far), (ids, scores, tokens, grads)
    copies = [
        pltpu.make_async_copy(source, target, done.at[n])
        for n, (source, target) in enumerate(zip(sources, targets))
    ]
    for copy in copies:
        copy.start()
    count = ids.shape[1]
    lanes = PARTS * count
    own_slots = slots // CORES
    each = PARTS * own_slots
    rows = groups * each
    expert = iota((rows, count), 0) // each * per_group + lax.axis_index("y")
    wide = iota((count, lanes), 1) % count
    at = iota((count, lanes), 0)
    ranker = jnp.where(at < wide, 1.0, jnp.where(at == wide, float(LATE), 0.0)).astype(BF16)
    row = iota((rows, lanes), 0) % each
    here = row // own_slots == iota((rows, lanes), 1) // count
    wanted = (row % own_slots + (LATE + own_slots * lax.axis_index("core"))).astype(F32)
    copies[0].wait()
    copies[1].wait()
    hit = jnp.zeros((rows, count), F32)
    score = jnp.zeros((rows, count), F32)
    for e in range(ids.shape[0]):
        same = ids[e : e + 1, :] == expert
        hit = jnp.where(same, 1.0, hit)
        score = jnp.where(same, scores[e : e + 1, :].astype(F32), score)
    rank = dot(hit.astype(BF16), ranker)
    found = rank == wanted
    mark = jnp.where(found & here, 1.0, 0.0).astype(BF16)
    slot_score = jnp.sum(jnp.where(found[:, :count], score, 0.0), axis=1, keepdims=True)
    part = tokens.shape[1] // PARTS
    copies[2].wait()
    out[:, :part] = dot(mark, stacked_parts(tokens)).astype(BF16)
    copies[3].wait()
    out[:, part:] = (slot_score * dot(mark, stacked_parts(grads))).astype(BF16)


ENTRIES = ((0, 0), (0, 1), (0, 2), (1, 2), (1, 3), (1, 4))
PIECE = 16


def describe(groups, per_group, slots, ids, gather, place, order):
    ids_now = ids[...]
    tokens = ids_now.shape[1]
    experts = groups * per_group
    hit = picked(ids_now, iota((experts, tokens), 0)) > 0.5
    rank = dot(hit.astype(BF16), before(tokens, tokens))
    code = jnp.where(hit, rank, -1.0).astype(BF16)
    lanes = experts * PIECE
    piece = iota((experts, lanes), 1) // PIECE
    expert = piece % groups * per_group + piece // groups
    widen = (expert == iota((experts, lanes), 0)).astype(BF16)
    spread = dot_first(code, widen).astype(jnp.int32)
    row = iota((tokens, lanes), 1) % PIECE
    for n, (odd, part) in enumerate(ENTRIES):
        mark = (spread == 2 * (row % 3) + odd) & (row // 3 == part)
        gather[n * tokens : (n + 1) * tokens, :] = mark.astype(BF16)

    own_slots = slots // CORES
    rows = groups * own_slots
    at, col = iota(place.shape, 0), iota(place.shape, 1)
    tall = place.shape[1] // (len(ENTRIES) * CORES)
    row, source = at % PIECE, col % tall
    slot = source % own_slots + col // tall % CORES * own_slots
    mark = jnp.zeros(place.shape, jnp.bool_)
    for n, (odd, part) in enumerate(ENTRIES):
        mark |= (col // (CORES * tall) == n) & (row // 3 == part) & (slot == 2 * (row % 3) + odd)
    place[...] = (mark & (at // PIECE == source // own_slots) & (source < rows)).astype(BF16)

    span = order.shape[1] // PARTS
    at, here = iota(order.shape[1:], 0), iota(order.shape[1:], 1)
    for h in range(2):
        inner = at % span + h * (tall - span - rows // 2)
        source = inner // own_slots * (PARTS * own_slots) + at // span * own_slots + inner % own_slots
        order[h] = ((source == here) & (inner >= 0) & (inner < rows // 2)).astype(BF16)


def round_up(n, k):
    return -(-n // k) * k


def backward(homes, tall, order, halves, ready, pairs, downs, write, ins, grads):
    span = order.shape[1] // PARTS
    apart = tall - span
    wide = ins.shape[2]
    part = wide // 2
    for k in range(len(homes)):
        a, b = dot(order[0], halves[2 * k]), dot(order[1], halves[2 * k + 1])
        for f in range(PARTS):
            at = f * span
            seam = a[at + apart : at + span] + b[at : at + span - apart]
            block = [a[at : at + apart], seam, b[at + span - apart : at + span]]
            block = jnp.concatenate(block, axis=0).astype(BF16)
            rows, lanes = slice(k * tall, (k + 1) * tall), slice(f % 2 * part, (f % 2 + 1) * part)
            ins[f // 2, rows, lanes] = block[:, :part]
            grads[f // 2, rows, lanes] = block[:, part:]
    for copy in ready:
        copy.wait()
    hidden = downs.shape[0] // CORES
    count = ins.shape[1]
    pre = jnp.zeros((2 * CORES * hidden, count), F32)
    act = jnp.zeros((CORES * hidden, count), F32)
    for f in range(PARTS // 2):
        lanes = slice(f * wide, (f + 1) * wide)
        pre += dot_last(pairs[:, lanes], ins[f])
        act += dot_last(downs[:, lanes], grads[f])
    parts = []
    for s in range(CORES):
        gate, up = pre[2 * s * hidden :][:hidden], pre[(2 * s + 1) * hidden :][:hidden]
        slope = act[s * hidden :][:hidden]
        sig = jax.nn.sigmoid(gate)
        parts.append(slope * up * sig * (1.0 + gate * (1.0 - sig)))
        parts.append(slope * gate * sig)
    hid = jnp.concatenate(parts, axis=0).T.astype(BF16)
    low = iota((count, LANES), 1) < LANES // 2

    def join(left, right):
        return jnp.where(low, left, right)

    def turn(x):
        return pltpu.roll(x, LANES // 2, 1)

    for f in range(pairs.shape[1] // (10 * LANES)):
        tiles = []
        for y in (2 * f, 2 * f + 1):
            lanes = slice(5 * LANES * y, 5 * LANES * (y + 1))
            total = dot(hid, pairs[:, lanes])
            tiles.append([total[:, t * LANES : (t + 1) * LANES] for t in range(5)])
        a, b = tiles
        at = [turn(a[t]) for t in (2, 3, 4)]
        bt = [turn(b[t]) for t in (0, 1, 2)]
        first = [a[0], a[1], join(a[2], bt[0]), join(bt[0], bt[1]), join(bt[1], bt[2])]
        second = [join(at[0], at[1]), join(at[1], at[2]), join(at[2], b[2]), b[3], b[4]]
        for core, group in enumerate((first, second)):
            for t, tile in enumerate(group):
                for k, home in enumerate(homes):
                    write(home, core, 5 * f + t, tile[k * tall : (k + 1) * tall])


def home_of(shift, members):
    return lax.rem(lax.axis_index("member") + shift, members)


def paired(rows, store):
    held = {}

    def write(home, core, t, tile):
        if t % 2 == 0:
            held[id(home), core] = tile
            return
        first = held.pop((id(home), core))
        extra = 2 * (tile.shape[0] - rows)
        last = pltpu.roll(tile, tile.shape[0] - rows, 0)
        stop = tile.shape[0] - extra
        parts = (first[:stop], first[stop:] + last[:extra], last[extra:])
        begin = t // 2 * 2 * rows
        for part in parts:
            store(home, core, begin, part.astype(BF16))
            begin += part.shape[0]

    return write


def backward_near(members, tall, rows, order, near, *refs):
    parts, weights, (out, pairs, downs, ins, grads, done) = refs[:4], refs[4:8], refs[8:]
    deep, flat = pairs.shape[0] // CORES, downs.shape[0] // CORES
    targets = (pairs.at[:deep], pairs.at[deep:], downs.at[:flat], downs.at[flat:])
    copies = [
        pltpu.make_async_copy(source, target, done.at[n])
        for n, (source, target) in enumerate(zip(weights, targets))
    ]
    for copy in copies:
        copy.start()
    middle = order.shape[2]
    halves = [near[:middle, :], near[middle:, :]] + [p[...] for p in parts]

    def store(home, core, begin, part):
        out[home * CORES + core, begin : begin + part.shape[0], :] = part

    turn = (members - 2) * lax.axis_index("core")
    homes = [home_of(shift, members) for shift in (0, members - 1 - turn, 1 + turn)]
    backward(homes, tall, order, halves, copies, pairs, downs, paired(rows, store), ins, grads)


def backward_opposite(members, tall, rows, order, top, bottom, pairs, downs, *refs):
    out, ins, grads, held, sent = refs[1:]
    home = home_of(members // 2, members)
    chunk = held.shape[1] // sent.shape[1]
    copies = []

    def store(_, core, begin, part):
        end = begin + part.shape[0]
        held[core, begin:end, :] = part
        if end % chunk == 0:
            at = pl.ds(end - chunk, chunk)
            copy = pltpu.make_async_copy(
                held.at[core, at], out.at[home * CORES + core, at], sent.at[core, end // chunk - 1]
            )
            copy.start()
            copies.append(copy)

    halves = [top[...], bottom[...]]
    backward([home], tall, order, halves, [], pairs, downs, paired(rows, store), ins, grads)
    for copy in copies:
        copy.wait()


def total_pieces(groups, columns, tall, rows, place, x, out):
    low = iota((tall, LANES), 1) < LANES // 2
    members = x.shape[0] // CORES
    for y in range(columns):
        sorted_entries = [[] for _ in ENTRIES]
        for c in range(CORES):
            tiles, turned = [], []
            for t in range(3):
                number = 5 * y // 2 + t
                at = number // 2 * 2 * rows + number % 2 * (2 * rows - tall)
                tile = x[c, at : at + tall, :].astype(F32)
                for m in range(1, members):
                    tile += x[m * CORES + c, at : at + tall, :].astype(F32)
                if number % 2 == 1:
                    tile = pltpu.roll(tile, rows, 0)
                tiles.append(tile)
                turned.append(pltpu.roll(tile, LANES // 2, 1))
            first = [
                jnp.where(low, turned[0], turned[1]),
                jnp.where(low, turned[1], turned[2]),
            ]
            if y % 2 == 0:
                seam = [jnp.where(low, tiles[2], 0.0), jnp.where(low, 0.0, turned[0])]
                entries = tiles[:2] + seam + first
            else:
                seam = [jnp.where(low, turned[2], 0.0), jnp.where(low, 0.0, tiles[0])]
                entries = first + seam + tiles[1:]
            for n, entry in enumerate(entries):
                sorted_entries[n].append(entry)
        stack = jnp.concatenate([e for pair in sorted_entries for e in pair], axis=0)
        moved = dot(place[...], stack.astype(BF16)).astype(BF16)
        for g in range(groups):
            out[y * groups + g] = moved[g * PIECE : (g + 1) * PIECE]


def finish(gather, x, out):
    tokens, chunk = out.shape
    found = dot(gather[...], x[...])
    part = [found[n * tokens : (n + 1) * tokens] for n in range(len(ENTRIES))]
    turned = [pltpu.roll(p, LANES // 2, 1) for p in part[3:]]
    low = iota((tokens, LANES), 1) < LANES // 2
    out[:, :LANES] = (part[0] + jnp.where(low, turned[0], turned[1])).astype(BF16)
    out[:, LANES : 2 * LANES] = (part[1] + jnp.where(low, turned[1], turned[2])).astype(BF16)
    last = (part[2] + turned[2]).astype(BF16)
    out[:, 2 * LANES :] = last[:, : chunk - 2 * LANES]


def per_device(tokens_in, out_grad, scores, expert_ids, w_in, w_down):
    groups, members = lax.axis_size("group"), lax.axis_size("member")
    columns = lax.axis_size("y")
    tokens, width = tokens_in.shape
    picks = expert_ids.shape[1]
    pairs = picks // TGROUPS
    slots = pairs * (TGROUPS * tokens // groups) // columns
    part = width // PARTS
    chunk = width // (CORES * columns)
    hidden = w_down.shape[1]
    block_rows = groups * slots // CORES
    tall, span = round_up(block_rows, 8), round_up(block_rows // 2, 8)
    packed_rows = block_rows * PARTS
    middle = packed_rows // 2

    def struct(shape, kind):
        return jax.ShapeDtypeStruct(shape, kind)

    def exchange(x, axis):
        return lax.all_to_all(x, axis, split_axis=0, concat_axis=0, tiled=True)

    def shift(x, step):
        hops = [
            (CORES * i + c, CORES * ((i + step * (1 - 2 * c)) % members) + c)
            for i in range(members)
            for c in range(CORES)
        ]
        return lax.ppermute(x, ("member", "core"), hops)

    def up(x):
        return shift(x, 1)

    def down(x):
        return shift(x, -1)

    def far(x):
        return lax.ppermute(x, "core", [(0, 1), (1, 0)])

    def bind(body, *front):
        return lambda *refs: body(*front, *refs)

    ids = expert_ids.T
    sent = call(
        bind(pack, groups, columns, slots),
        struct((packed_rows, 2 * part), BF16),
        ids, scores.T, tokens_in, out_grad,
        far={i: pltpu.HBM for i in range(4)}, room=60,
        scratch=(
            pltpu.VMEM(ids.shape, ids.dtype),
            pltpu.VMEM(ids.shape, BF16),
            pltpu.VMEM((tokens, width), BF16),
            pltpu.VMEM((tokens, width), BF16),
            pltpu.SemaphoreType.DMA((4,)),
        ),
    )
    w_pair = w_in[0].reshape(2 * hidden, width)
    w_out = w_down[0]
    sent, ids, pair_late, out_late = lax.optimization_barrier((sent, ids, w_pair, w_out))
    near = exchange(sent.reshape(groups, -1, 2 * part), "group").reshape(sent.shape)
    pair_far, out_far = far(pair_late), far(out_late)
    gather, place, order = call(
        bind(describe, groups, columns, slots),
        (
            struct((len(ENTRIES) * tokens, groups * columns * PIECE), BF16),
            struct((groups * PIECE, len(ENTRIES) * CORES * tall), BF16),
            struct((2, PARTS * span, middle), BF16),
        ),
        ids,
    )
    near, order = lax.optimization_barrier((near, order))
    weights = (w_pair, pair_far, w_out, out_far)

    top, bottom = near[:middle], near[middle:]
    below_top, above_bottom = up(top), down(bottom)
    below_bottom = up(bottom)
    above_top = down(top)
    opposite = (up(below_top), down(above_bottom))

    lane_tiles = width // (CORES * LANES)
    result = struct((members * CORES, lane_tiles * block_rows, LANES), BF16)

    def rows(blocks):
        return pltpu.VMEM((PARTS // 2, blocks * tall, 2 * part), BF16)

    partial, pairs_all, downs_all = call(
        bind(backward_near, members, tall, block_rows),
        (
            result,
            struct((CORES * 2 * hidden, width), BF16),
            struct((CORES * hidden, width), BF16),
        ),
        order, near, below_top, below_bottom, above_top, above_bottom, *weights,
        far={6: pl.ANY, 7: pltpu.HBM, 8: pl.ANY, 9: pltpu.HBM},
        flops=2 * 3 * tall * width * 10 * hidden,
        scratch=(rows(3), rows(3), pltpu.SemaphoreType.DMA((4,))),
    )
    partial = call(
        bind(backward_opposite, members, tall, block_rows),
        result,
        order, *opposite, pairs_all, downs_all, partial,
        far={5: pl.ANY}, far_out=True, alias=5,
        flops=2 * tall * width * 10 * hidden,
        scratch=(
            rows(1),
            rows(1),
            pltpu.VMEM((CORES,) + result.shape[1:], BF16),
            pltpu.SemaphoreType.DMA((CORES, lane_tiles // 10)),
        ),
    )
    pieces = call(
        bind(total_pieces, groups, columns, tall, block_rows),
        struct((groups * columns, PIECE, LANES), BF16),
        place, exchange(partial, ("member", "core")),
    )
    arrived = exchange(pieces, ("y", "group")).reshape(-1, LANES)
    return call(finish, struct((tokens, chunk), BF16), gather, arrived)


def solution(mesh):
    shape = mesh.devices.shape
    split = Mesh(
        mesh.devices.reshape(shape[0], shape[1], shape[2] // 2, 2),
        ("group", "member", "y", "core"),
    )
    in_specs = (
        P(("group", "member"), None),
        P(("group", "member"), None),
        P(("group", "member"), None),
        P(("group", "member"), None),
        P(("group", "y", "core"), None, "member", None),
        P(("group", "y", "core"), "member", None),
    )
    out_specs = P(("group", "member"), ("y", "core"))
    return jax.shard_map(
        per_device, mesh=split, in_specs=in_specs, out_specs=out_specs, check_vma=False
    )
```
